256 devices in a mesh: tm: 64 (over z, y, core), sensor: 4 (over x).
Axes of the slice: x: 4, y: 4, z: 8, core: 2. Of those that a mesh axis runs over, the one named last changes fastest.
Arguments:
- observations: bfloat16 [16384, 16384], P(('sensor', 'tm')), may hold values from -6 to 6
- sensor_map: bfloat16 [16384, 128], P('sensor'), may hold values from -0.046875 to 0.046875
- noise_precision: bfloat16 [128, 128, 128], P('sensor'), may hold values from -0.0031496063 to 1.4, as said below
- availability: int32 [64, 128], P('tm', 'sensor'), may hold values from 0 to 1
- decay_rate: float32 [128], replicated, may hold values from 6.1035157e-06 to 0.03
- prior_mean: float32 [128], replicated, may hold values from -6 to 6
Outputs:
- filtered_states: float32 [16384, 128], P('tm')
The draws below stay inside these ranges and needn't reach their ends.
Inputs may be any that keep to these rules, and one draw needn't show every extreme that they name: `noise_precision`: each block is symmetric, its diagonal lies in 0.6 to 1.4 and exceeds the sum of magnitudes of the rest of its row.
All inputs are finite; a program needn't handle non-finite values.
Results may differ from the reference program's by a relative error of at most 0.0019.
Values may be sent and summed in bfloat16 or wider, within the bound.
No kernel may reach another device: no remote copies, remote signals or barrier semaphores. Data moves between devices by JAX's collectives and lax.ppermute only.
A program may use at most 128 MiB of HBM per device.

```python
import math
import jax
import jax.numpy as jnp
from jax import lax

MODES = 128
SENSORS = 16384
SBLK = 128
TB_DEV = 256
T_WIN = 16384
NBLK = 128
N_TM = 64


def draw_noise_precision(key, part):
    key_off, key_diag = jax.random.split(jax.random.fold_in(key, 7))
    off_part = jax.random.uniform(key_off, (NBLK, SBLK, SBLK), jnp.float32, -1.0, 1.0)
    off_part = 0.5 * (off_part + jnp.swapaxes(off_part, 1, 2)) * (0.4 / (SBLK - 1))
    diag_part = jax.random.uniform(key_diag, (NBLK, SBLK), jnp.float32, 0.6, 1.4)
    identity = jnp.eye(SBLK, dtype=jnp.float32)
    return (off_part * (1.0 - identity) + identity * diag_part[:, :, None]).astype(jnp.bfloat16)


def draw_availability(key, part):
    key = jax.random.fold_in(key, 11)
    key_level, key_pick, key_start, key_length = jax.random.split(key, 4)
    rate_level = jax.random.randint(key_level, (N_TM, 1), 2, 9)
    sensor_pick = jax.random.randint(key_pick, (N_TM, NBLK), 0, 8)
    run_start = jax.random.randint(key_start, (1, NBLK), 0, N_TM)
    run_length = jax.random.randint(key_length, (1, NBLK), max(N_TM // 4, 1), N_TM // 2 + 1)
    block_steps = jnp.arange(N_TM, dtype=jnp.int32)[:, None]
    silent_run = (block_steps >= run_start) & (block_steps < run_start + run_length)
    reporting = (sensor_pick < rate_level) & jnp.logical_not(silent_run)
    return jnp.where(reporting, 1, 0).astype(jnp.int32)


def level_of(stream_key, extent, cuts, low, top_value):
    def one(dim, parts):
        draws = jax.random.uniform(jax.random.fold_in(jax.random.fold_in(stream_key, 6), dim), (parts,), jnp.float32, low / len(cuts), top_value / len(cuts))
        return jnp.repeat(jnp.exp(draws), extent[dim] // parts).reshape((-1,) + (1,) * (len(extent) - dim - 1))

    loudness = one(*cuts[0])
    for cut in cuts[1:]:
        loudness = loudness * one(*cut)
    return loudness


def gaussian(rng, extent, deviation, limit, cuts=(), held_as=jnp.bfloat16):
    level = level_of(rng, extent, cuts, -0.22, 0.18) if cuts else 1.0
    result = jax.random.normal(rng, extent, jnp.float32) * deviation * level
    return jnp.minimum(jnp.maximum(result, -limit), limit).astype(held_as)


def setup_inputs(seed: int = 0) -> dict:
    seeds = jax.random.split(jax.random.key(seed), 7)
    observations = gaussian(seeds[0], (SENSORS, T_WIN), 1.0, 6.0, ((0, 256),))
    sensor_map = gaussian(seeds[1], (SENSORS, MODES), SENSORS ** -0.5, 0.046875, ((0, 4),))
    noise_precision = draw_noise_precision(jax.random.fold_in(seeds[6], 71), 0)
    availability = draw_availability(jax.random.fold_in(seeds[6], 71), 0)
    decay_rate = jnp.clip(jnp.exp(jax.random.uniform(seeds[4], (MODES,), jnp.float32, math.log(6.10351571594947e-06), math.log(0.03))), 6.10351571594947e-06, 0.03)
    prior_mean = gaussian(seeds[5], (MODES,), 1.0, 6.0, (), jnp.float32)
    return dict(observations=observations, sensor_map=sensor_map, noise_precision=noise_precision, availability=availability, decay_rate=decay_rate, prior_mean=prior_mean)


def sweep_rows(rows, powers):
    for level in range(len(powers)):
        offset = 2 ** level
        moved = jnp.dot(rows[:-offset], powers[level].T, precision=lax.Precision.HIGHEST)
        rows = rows + jnp.pad(moved, ((offset, 0), (0, 0)))
    return rows


def reference(observations, sensor_map, noise_precision, availability, decay_rate, prior_mean):
    block_count = SENSORS // SBLK
    weighted = jnp.einsum("bij,bjm->bim", noise_precision.astype(jnp.float32), sensor_map.reshape(block_count, SBLK, MODES).astype(jnp.float32), precision=lax.Precision.HIGHEST)
    weighted = weighted.astype(jnp.bfloat16).reshape(SENSORS, MODES)
    retain = jnp.exp(-decay_rate)
    identity = jnp.eye(MODES, dtype=jnp.float32)
    contract = (((0,), (0,)), ((), ()))
    levels = TB_DEV.bit_length() - 1

    def one_block(state, block_index):
        kept_blocks = jnp.repeat(availability[block_index].astype(jnp.bfloat16), SBLK)
        masked = weighted * kept_blocks[:, None]
        window_obs = lax.dynamic_slice_in_dim(observations, block_index * TB_DEV, TB_DEV, 1)
        info_rows = lax.dot_general(window_obs, masked, contract, preferred_element_type=jnp.float32)
        info_matrix = lax.dot_general(sensor_map, masked, contract, preferred_element_type=jnp.float32)
        transition = (identity - decay_rate[:, None] * info_matrix) * retain[None, :]
        drive = decay_rate[None, :] * info_rows
        powers = []
        current_power = transition
        for level in range(levels):
            powers.append(current_power)
            current_power = jnp.dot(current_power, current_power, precision=lax.Precision.HIGHEST)
        start_push = jnp.dot(transition, state, precision=lax.Precision.HIGHEST)
        states = sweep_rows(drive.at[0].add(start_push), powers)
        return states[-1], states

    final_state, all_states = lax.scan(one_block, prior_mean.astype(jnp.float32), jnp.arange(N_TM, dtype=jnp.int32))
    return all_states.reshape(T_WIN, MODES)
```

```python
import jax
import jax.numpy as jnp
import numpy as np
from jax import lax
from jax.sharding import Mesh, PartitionSpec as P

NZ, NY, NC, NX = 8, 4, 2, 4
BLOCK_AXES = ("y", "c")
HIGHEST = lax.Precision.HIGHEST


def dot(a, b):
    return jnp.dot(a, b, precision=HIGHEST)


def xor_over_x(block, distance):
    return lax.ppermute(block, "x", [(i, i ^ distance) for i in range(NX)])


def sum_over_x(block):
    first, second, third = (xor_over_x(block, d) for d in (1, 2, 3))
    return (block + first) + (second + third)


def in_order_of_x(blocks, x):
    stacked = jnp.stack(blocks)
    return jnp.stack([lax.dynamic_index_in_dim(stacked, g ^ x, 0, False) for g in range(NX)])


def rows_to_block(piece, distance):
    route = []
    for z in range(NZ):
        for x in range(NX):
            part = 2 * (x // 2) + z % 2
            route.append((z * NX + x, (z // 2 * 2 + x % 2) * NX + (part ^ distance)))
    return lax.ppermute(piece, ("z", "x"), route)


def on_device(observations, sensor_map, noise_precision, availability, decay_rate, prior_mean):
    modes = sensor_map.shape[1]
    sblk = noise_precision.shape[1]
    rows = observations.shape[0]
    z, y, c, x = (lax.axis_index(a) for a in "zycx")
    place = y * NC + c

    sent = observations.reshape(rows, NZ // 2, 2, NY, NC, 2, 128)
    sent = sent.transpose(3, 4, 5, 2, 0, 1, 6).reshape(NY * NC * NX, rows, NZ // 2 * 128)
    received = lax.all_to_all(sent, ("y", "c", "x"), split_axis=0, concat_axis=0, tiled=True)

    weighted = jnp.einsum(
        "bij,bjm->bim",
        noise_precision,
        sensor_map.reshape(-1, sblk, modes),
        preferred_element_type=jnp.float32,
    ).astype(jnp.bfloat16)
    kept = availability[0].astype(jnp.bfloat16)
    masked_own = (weighted * kept[:, None, None]).reshape(-1, modes)
    contract = (((0,), (0,)), ((), ()))
    info_matrix = sum_over_x(
        lax.dot_general(sensor_map, masked_own, contract, preferred_element_type=jnp.float32)
    )

    kept_plane = lax.all_to_all(kept.reshape(NZ, -1), "z", split_axis=0, concat_axis=0, tiled=True)
    plane = lax.dynamic_slice_in_dim(weighted.reshape(-1, modes), z * NY * sblk, NY * sblk)
    label = jnp.zeros((16, modes), jnp.bfloat16).at[:NZ, :NY].set(kept_plane)
    packet = jnp.concatenate([plane, label], 0)
    packets = in_order_of_x([packet] + [xor_over_x(packet, d) for d in (1, 2, 3)], x)
    plane = packets[:, : NY * sblk].reshape(NX, NY, NC, rows, modes).transpose(1, 2, 0, 3, 4)
    kept_all = packets[:, NY * sblk : NY * sblk + NZ, :NY].reshape(NX, NZ // 2, 2, NY)
    kept_all = lax.dynamic_index_in_dim(kept_all, x % 2, 2, False)
    masked = plane[None] * kept_all.transpose(1, 2, 0)[:, :, None, :, None, None]
    masked = masked.reshape(NZ // 2, -1, modes)

    retain = jnp.exp(-decay_rate)
    identity = jnp.eye(modes, dtype=jnp.float32)
    transition = (identity - decay_rate[:, None] * info_matrix) * retain[None, :]
    powers = [transition]
    for _ in range(8):
        powers.append(dot(powers[-1], powers[-1]))
    blocks = lax.all_gather(powers[8], BLOCK_AXES)
    suffix, own_suffix = identity, identity
    for j in reversed(range(NY * NC)):
        own_suffix = jnp.where(place == j, suffix, own_suffix)
        suffix = dot(suffix, blocks[j])
    plane_product = suffix
    planes = lax.all_gather(plane_product, "z")
    lead, within = identity, []
    for j in reversed(range(NY * NC)):
        before = j < place
        within.append(jnp.where(before, lead, 0.0))
        lead = jnp.where(before, dot(lead, blocks[j]), lead)
    across = []
    for j in reversed(range(NZ)):
        before = j < z
        across.append(jnp.where(before, lead, 0.0))
        lead = jnp.where(before, dot(lead, planes[j]), lead)
    to_entry = jnp.concatenate(across[::-1] + within[::-1], 1)
    from_prior = dot(lead, prior_mean)

    partial = jnp.einsum(
        "kmt,mkn->mtn",
        received.reshape(-1, NZ // 2, 128),
        masked,
        preferred_element_type=jnp.float32,
    )
    partial = partial.reshape(NZ, -1, modes)
    piece = jnp.sum(lax.all_to_all(partial, "z", split_axis=0, concat_axis=0, tiled=True), 0)
    pieces = in_order_of_x([rows_to_block(piece, d) for d in range(NX)], x)
    drive = decay_rate[None, :] * pieces.reshape(-1, modes)

    tail = drive
    for level in range(8):
        tail = tail.reshape(-1, 2, modes)
        tail = dot(tail[:, 0], powers[level].T) + tail[:, 1]
    offset = tail[0]
    onward = dot(own_suffix, offset)
    same_plane = (jnp.arange(NZ) == z)[:, None, None]
    sends = jnp.broadcast_to(
        jnp.where(same_plane, offset[None, None], onward[None, None]), (NZ, NY * NC, modes)
    ).reshape(-1, modes)
    offsets = lax.all_to_all(sends, ("z", "y", "c"), split_axis=0, concat_axis=0, tiled=True)
    offsets = offsets.reshape(NZ, NY * NC, modes)
    own_plane = lax.dynamic_index_in_dim(offsets, z, 0, False)
    vector = jnp.concatenate([jnp.sum(offsets, 1).reshape(-1), own_plane.reshape(-1)])
    entry = from_prior + dot(to_entry, vector)

    swept = drive
    for level in range(8):
        shift = 2**level
        moved = dot(swept[:-shift], powers[level].T)
        swept = swept + jnp.pad(moved, ((shift, 0), (0, 0)))
    grown = dot(entry[None, :], transition.T)
    for level in range(8):
        grown = jnp.concatenate([grown, dot(grown, powers[level].T)], 0)
    return swept + grown


def solution(mesh):
    fine = Mesh(mesh.devices.reshape(NZ, NY, NC, NX), ("z", "y", "c", "x"))
    return jax.shard_map(
        on_device,
        mesh=fine,
        in_specs=(
            P(("x", "z", "y", "c"), None),
            P("x", None),
            P("x", None, None),
            P(("z", "y", "c"), "x"),
            P(),
            P(),
        ),
        out_specs=P(("z", "y", "c"), None),
        check_vma=False,
    )
```

```python
import jax
import jax.numpy as jnp
from jax import lax
from jax.experimental import pallas as pl
from jax.experimental.pallas import tpu as pltpu
from jax.sharding import Mesh, PartitionSpec as P

NZ, NY, NC, NX = 8, 4, 2, 4
NK = NZ * NY * NC
STEPS = 256
LEVELS = 8
SCAN = 6
LANES = 128
TAKERS = NY * NC * 2
HIGHEST = lax.Precision.HIGHEST
WHOLE = pl.BlockSpec(memory_space=pltpu.VMEM)
SCALARS = pl.BlockSpec(memory_space=pltpu.SMEM)


def dot(a, b):
    return jnp.dot(a, b, precision=HIGHEST, preferred_element_type=jnp.float32)


def f32(*shape):
    return jax.ShapeDtypeStruct(shape, jnp.float32)


def local(body, name, scalars, arrays, outs, flops, tokens=(), scratch=(), moved=1 << 20):
    inputs = len(scalars) + len(arrays)

    def call(*refs):
        body(*refs[:inputs], *refs[inputs + len(tokens) :])

    return pl.pallas_call(
        call,
        name=name,
        out_shape=outs,
        in_specs=[SCALARS] * len(scalars)
        + [WHOLE] * (len(arrays) + len(tokens)),
        out_specs=[WHOLE] * len(outs),
        scratch_shapes=list(scratch),
        cost_estimate=pl.CostEstimate(flops=flops, bytes_accessed=moved, transcendentals=0),
        compiler_params=pltpu.CompilerParams(vmem_limit_bytes=32 << 20),
    )(*scalars, *arrays, *tokens)


def split(a):
    high = a.astype(jnp.bfloat16)
    return high, (a - high.astype(jnp.float32)).astype(jnp.bfloat16)


def wide(a):
    high, low = split(a)
    return jnp.concatenate([high, low, high], 1)


def tall(a):
    high, low = split(a)
    return jnp.concatenate([high, high, low], 0)


def times(terms, factor):
    return jnp.dot(terms, factor, preferred_element_type=jnp.float32)


def xor_over_x(block, distance):
    return lax.ppermute(block, "x", [(i, i ^ distance) for i in range(NX)])


def rows_to_block(piece, distance):
    route = []
    for z in range(NZ):
        for x in range(NX):
            part = 2 * (x // 2) + z % 2
            route.append((z * NX + x, (z // 2 * 2 + x % 2) * NX + (part ^ distance)))
    return lax.ppermute(piece, ("z", "x"), route)


def order_kernel(rows_ref, *refs):
    out_ref = refs[-1]
    for m in range(NZ // 2):
        for par in range(2):
            for j in range(TAKERS):
                lane = ((m * 2 + par) * TAKERS + j) * LANES
                out_ref[j, par, m] = rows_ref[:, lane : lane + LANES]


def by_taker(observations, *tokens):
    rows = observations.shape[0]
    out = pl.pallas_call(
        order_kernel,
        name="by_taker",
        out_shape=jax.ShapeDtypeStruct((TAKERS, 2, NZ // 2, rows, LANES), jnp.bfloat16),
        in_specs=[WHOLE] * (1 + len(tokens)),
        out_specs=WHOLE,
        cost_estimate=pl.CostEstimate(flops=0, bytes_accessed=4 << 20, transcendentals=0),
        compiler_params=pltpu.CompilerParams(vmem_limit_bytes=32 << 20),
    )(observations, *tokens)
    return out.reshape(TAKERS * 2, NZ // 2 * rows, LANES)


def pack_kernel(kept_ref, noise_ref, map_ref, out_ref, noise_held, map_held, sems):
    first = lax.axis_index("z") * NY + lax.axis_index("c") * 2
    copies = [
        pltpu.make_async_copy(noise_ref.at[pl.ds(first, 2)], noise_held, sems.at[0]),
        pltpu.make_async_copy(map_ref.at[pl.ds(first * LANES, 2 * LANES)], map_held, sems.at[1]),
    ]
    for copy in copies:
        copy.start()
    blocks = kept_ref.shape[1]
    lane = lax.broadcasted_iota(jnp.int32, (16, LANES), 1) - lax.axis_index("x") * blocks
    row = jnp.zeros((16, LANES), jnp.float32)
    for b in range(blocks):
        row = jnp.where(lane == b, kept_ref[0, b].astype(jnp.float32), row)
    out_ref[LANES:, :LANES] = row.astype(jnp.bfloat16)
    out_ref[LANES:, LANES:] = jnp.zeros((16, LANES), jnp.bfloat16)
    for copy in copies:
        copy.wait()
    for b in range(2):
        weights = jnp.dot(
            noise_held[b], map_held[b * LANES : (b + 1) * LANES, :], preferred_element_type=jnp.float32
        )
        out_ref[:LANES, b * LANES : (b + 1) * LANES] = weights.T.astype(jnp.bfloat16)


def pack(availability, noise_precision, sensor_map):
    return pl.pallas_call(
        pack_kernel,
        name="pack",
        out_shape=jax.ShapeDtypeStruct((LANES + 16, 2 * LANES), jnp.bfloat16),
        in_specs=[SCALARS, pl.BlockSpec(memory_space=pl.ANY), pl.BlockSpec(memory_space=pl.ANY)],
        out_specs=WHOLE,
        scratch_shapes=[
            pltpu.VMEM((2, LANES, LANES), jnp.bfloat16),
            pltpu.VMEM((2 * LANES, LANES), jnp.bfloat16),
            pltpu.SemaphoreType.DMA((2,)),
        ],
        cost_estimate=pl.CostEstimate(flops=1 << 23, bytes_accessed=1 << 18, transcendentals=0),
    )(availability, noise_precision, sensor_map)


def gather_kernel(place_ref, own_ref, one_ref, two_ref, three_ref, kept_ref, half_ref):
    refs = (own_ref, one_ref, two_ref, three_ref)
    kept = sum(ref[LANES:, :LANES].astype(jnp.float32)[:NZ] for ref in refs)
    at = lax.broadcasted_iota(jnp.int32, (NZ, LANES), 0)
    kept_ref[...] = jnp.where(at == place_ref[2], kept, 0.0)
    for r, ref in enumerate(refs):
        half_ref[:, 2 * r * LANES : 2 * (r + 1) * LANES] = ref[:LANES]


def weigh_kernel(kept_ref, noise_ref, map_ref, out_ref):
    step = pl.program_id(0)
    blocks, sblk = noise_ref.shape[0], noise_ref.shape[1]
    parts = []
    for b in range(blocks):
        weights = jnp.dot(
            noise_ref[b], map_ref[b * sblk : (b + 1) * sblk, :], preferred_element_type=jnp.float32
        )
        parts.append((weights * kept_ref[0, step * blocks + b].astype(jnp.float32)).astype(jnp.bfloat16))
    share = lax.dot_general(
        jnp.concatenate(parts, 0), map_ref[...], (((0,), (0,)), ((), ())), preferred_element_type=jnp.float32
    )

    @pl.when(step == 0)
    def _():
        out_ref[...] = share

    @pl.when(step > 0)
    def _():
        out_ref[...] += share


def weigh(availability, noise_precision, sensor_map):
    blocks, sblk, _ = noise_precision.shape
    step = blocks // 4
    return pl.pallas_call(
        weigh_kernel,
        name="weigh",
        grid=(4,),
        out_shape=f32(LANES, LANES),
        in_specs=[
            SCALARS,
            pl.BlockSpec((step, sblk, sblk), lambda i: (i, 0, 0)),
            pl.BlockSpec((step * sblk, LANES), lambda i: (i, 0)),
        ],
        out_specs=pl.BlockSpec((LANES, LANES), lambda i: (0, 0)),
        cost_estimate=pl.CostEstimate(flops=4 * blocks * sblk**3, bytes_accessed=2 << 20, transcendentals=0),
    )(availability, noise_precision, sensor_map)


def power_kernel(own_ref, one_ref, two_ref, three_ref, decay_ref, retain_ref, out_ref, block_ref):
    info = (own_ref[...] + one_ref[...]) + (two_ref[...] + three_ref[...])
    row = lax.broadcasted_iota(jnp.int32, info.shape, 0)
    column = lax.broadcasted_iota(jnp.int32, info.shape, 1)
    identity = jnp.where(row == column, 1.0, 0.0)
    power = (identity - decay_ref[...] * info) * retain_ref[...]
    for level in range(LEVELS):
        out_ref[level] = power
        power = dot(power, power)
    block_ref[...] = power


def factor_kernel(power_ref, add_ref, spread_ref):
    for step in range(LEVELS // 2):
        one, two = power_ref[2 * step], power_ref[2 * step + 1]
        for j, power in enumerate((one, two, dot(one, two))):
            terms = tall(power)
            add_ref[step, (2 - j) * 3 * LANES : (3 - j) * 3 * LANES] = terms
            spread_ref[step, :, j * LANES : (j + 1) * LANES] = terms


def joined(upper, total, beside, lead, rest):
    both = dot(jnp.where(upper, beside, total), jnp.where(upper, total, beside))
    new = dot(jnp.where(upper, beside, rest), jnp.where(upper, lead, beside))
    return both, jnp.where(upper, new, lead), jnp.where(upper, rest, new)


def pair_kernel(place_ref, total_ref, got_ref, total_out, lead_out, rest_out, lead_terms, rest_terms):
    row = lax.broadcasted_iota(jnp.int32, (LANES, LANES), 0)
    column = lax.broadcasted_iota(jnp.int32, (LANES, LANES), 1)
    identity = jnp.where(row == column, 1.0, 0.0)
    upper = place_ref[1] % 2 == 1
    total, got = total_ref[...], got_ref[...]
    lead, rest = jnp.where(upper, got, identity), jnp.where(upper, identity, got)
    total_out[...] = dot(jnp.where(upper, got, total), jnp.where(upper, total, got))
    lead_out[...], rest_out[...] = lead, rest
    lead_terms[...], rest_terms[...] = tall(lead), tall(rest)


def quad_kernel(bits_ref, total_ref, one_ref, two_ref, three_ref, lead_ref, rest_ref, total_out, lead_out, rest_out, *terms):
    odd, upper = bits_ref[0] % 2 == 1, bits_ref[0] % 4 >= 2
    two, three = two_ref[...], three_ref[...]
    total, lead, rest = joined(odd, total_ref[...], one_ref[...], lead_ref[...], rest_ref[...])
    terms[0][...], terms[1][...] = tall(lead), tall(rest)
    beside = dot(jnp.where(odd, three, two), jnp.where(odd, two, three))
    total, lead, rest = joined(upper, total, beside, lead, rest)
    terms[2][...], terms[3][...] = tall(lead), tall(rest)
    total_out[...], lead_out[...], rest_out[...] = total, lead, rest


def mask_kernel(place_ref, kept_ref, own_ref, other_ref, plane_ref, mask_ref):
    x, z, c = place_ref[0], place_ref[2], place_ref[3]
    half = NZ // 2
    zs = lax.broadcasted_iota(jnp.int32, (NZ, NZ), 1)
    pick = lax.broadcasted_iota(jnp.int32, (NZ, NZ), 0) * 2 + x % 2
    kept = jnp.dot(
        jnp.where(zs == pick, 1.0, 0.0).astype(jnp.bfloat16),
        kept_ref[...].astype(jnp.bfloat16),
        preferred_element_type=jnp.float32,
    ).astype(jnp.bfloat16)
    width = NY * LANES
    block = lax.broadcasted_iota(jnp.int32, (LANES, width), 0)
    lane = lax.broadcasted_iota(jnp.int32, (LANES, width), 1) // LANES
    for r in range(NX):
        own, other = own_ref[:, r * width // 2 : (r + 1) * width // 2], other_ref[:, r * width // 2 : (r + 1) * width // 2]
        plane_ref[:, r * width : r * width + width // 2] = jnp.where(c == 0, own, other)
        plane_ref[:, r * width + width // 2 : (r + 1) * width] = jnp.where(c == 0, other, own)
        spread = jnp.where(block == (x ^ r) * (NZ * NY) + z * NY + lane, 1.0, 0.0).astype(jnp.bfloat16)
        mask_ref[:, r * width : (r + 1) * width] = jnp.dot(kept, spread, preferred_element_type=jnp.float32)


def rows_kernel(place_ref, mask_ref, plane_ref, got_ref, one_ref, two_ref, three_ref, out_ref, token_ref, held_ref, sems):
    token_ref[...] = jnp.zeros((8, LANES), jnp.float32)
    x = place_ref[0]
    width = NY * LANES
    copies = [
        pltpu.make_async_copy(got_ref.at[:, :, m], held_ref.at[m], sems.at[m]) for m in range(NZ // 2)
    ]
    for copy in copies:
        copy.start()
    for m, copy in enumerate(copies):
        copy.wait()
        mask = mask_ref[m : m + 1, :].astype(jnp.bfloat16)
        weights = plane_ref[...] * mask
        readings = jnp.concatenate([held_ref[m, :, x ^ r].reshape(width, LANES) for r in range(NX)], 0)
        out_ref[m] = jnp.dot(weights, readings, preferred_element_type=jnp.float32).T


def info_rows(place, masks, plane, received, shares):
    takers, _, steps, rows, _ = received.shape
    return pl.pallas_call(
        rows_kernel,
        name="rows",
        out_shape=[f32(steps, LANES, LANES), f32(8, LANES)],
        in_specs=[SCALARS, WHOLE, WHOLE, pl.BlockSpec(memory_space=pl.ANY)] + [WHOLE] * 3,
        out_specs=[WHOLE] * 2,
        scratch_shapes=[
            pltpu.VMEM((steps, takers, NX, rows, LANES), jnp.bfloat16),
            pltpu.SemaphoreType.DMA((steps,)),
        ],
        cost_estimate=pl.CostEstimate(flops=1 << 28, bytes_accessed=3 << 20, transcendentals=0),
        compiler_params=pltpu.CompilerParams(vmem_limit_bytes=32 << 20),
    )(place, masks, plane, received, *shares)


def tail_kernel(place_ref, a_ref, b_ref, c_ref, d_ref, decay_ref, prior_ref, add_ref, spread_ref, drive_ref, tail_ref):
    x = place_ref[0]
    rows = a_ref.shape[0]
    for r, ref in enumerate((a_ref, b_ref, c_ref, d_ref)):
        drive_ref[pl.ds(pl.multiple_of((x ^ r) * rows, rows), rows), :] = ref[...] * decay_ref[...]
    pushed = times(wide(prior_ref[...]), spread_ref[0, :, :LANES])
    drive_ref[:1] += jnp.where(place_ref[1] == 0, pushed, 0.0)
    tail = drive_ref[...]
    for step in reversed(range(LEVELS // 2)):
        n = 4**step
        terms = jnp.concatenate([wide(tail[j * n : (j + 1) * n]) for j in range(3)], 1)
        tail = times(terms, add_ref[step]) + tail[3 * n :]
    tail_ref[...] = jnp.broadcast_to(tail, (8, LANES))


def send_kernel(place_ref, tail_ref, *refs):
    rest_refs, send_ref = refs[:-1], refs[-1]
    to = lax.broadcasted_iota(jnp.int32, (NK, LANES), 0) ^ place_ref[1]
    tail = tail_ref[...]
    terms = wide(tail)
    sends = jnp.broadcast_to(tail[:1], (NK, LANES))
    for level in range(1, SCAN):
        onward = times(terms, rest_refs[level - 1][...])
        sends = jnp.where(to >= 2**level, onward[:1], sends)
    send_ref[...] = sends


def sweep_kernel(drive_ref, spread_ref, out_ref):
    swept = drive_ref[...]
    row = lax.broadcasted_iota(jnp.int32, (STEPS, LANES), 0)
    for step in range(LEVELS // 2):
        for side in range(2):
            shift = 4**step * (1 + side)
            before = jnp.where(row >= shift, pltpu.roll(swept, shift, 0), 0.0)
            swept += times(wide(before), spread_ref[step, :, side * LANES : (side + 1) * LANES])
    out_ref[...] = swept


def state_kernel(place_ref, offsets_ref, spread_ref, swept_ref, *refs):
    lead_refs, out_ref = refs[:-1], refs[-1]
    k = place_ref[1]
    index = lax.broadcasted_iota(jnp.int32, (NK, LANES), 0)
    apart = jnp.where(index < k, index ^ k, 0)
    offsets = offsets_ref[...]
    parts = []
    for level in range(SCAN):
        chosen = (apart >= 2**level) & (apart < 2 ** (level + 1))
        parts.append(jnp.sum(jnp.where(chosen, offsets, 0.0), 0, keepdims=True))
    entry = parts[0]
    for level in range(1, SCAN):
        entry += times(wide(parts[level]), lead_refs[level - 1][...])
    grown = times(wide(entry), spread_ref[0, :, :LANES])
    for step in range(LEVELS // 2):
        more = times(wide(grown), spread_ref[step])
        grown = jnp.concatenate([grown] + [more[:, j * LANES : (j + 1) * LANES] for j in range(3)], 0)
    out_ref[...] = swept_ref[...] + grown


def on_device(observations, sensor_map, noise_precision, availability, decay_rate, prior_mean):
    modes = sensor_map.shape[1]
    rows = observations.shape[0]
    z, y, c, x = (lax.axis_index(a) for a in "zycx")
    k = (z * NY + y) * NC + c
    place = jnp.stack([x, k, z, c, y]).astype(jnp.int32)
    square = f32(modes, modes)
    packet = pack(availability, noise_precision, sensor_map)
    packets = [packet] + [xor_over_x(packet, d) for d in (1, 2, 3)]
    kept, half = local(
        gather_kernel, "gather", [place], packets,
        [f32(NZ, modes), jax.ShapeDtypeStruct((modes, NX * 2 * modes), jnp.bfloat16)], 1 << 16,
    )
    sent = by_taker(observations, *packets[1:])
    received = lax.all_to_all(sent, ("y", "c", "x"), split_axis=0, concat_axis=0, tiled=True)

    for flip in (1, 2, 4):
        kept = kept + lax.ppermute(kept, "z", [(i, i ^ flip) for i in range(NZ)])
    plane, masks = local(
        mask_kernel, "masks", [place], [kept, half, lax.ppermute(half, "c", [(0, 1), (1, 0)])],
        [jax.ShapeDtypeStruct((modes, NX * NY * modes), jnp.bfloat16), f32(NZ, NX * NY * modes)], 1 << 20,
    )

    info = weigh(availability, noise_precision, sensor_map)
    infos = [info] + [xor_over_x(info, d) for d in (1, 2, 3)]

    partial, done = info_rows(place, masks, plane, received.reshape(NY * NC, NX, NZ // 2, rows, LANES), infos[1:])
    partial = lax.all_to_all(partial.reshape(NZ, -1, modes), "z", split_axis=0, concat_axis=0, tiled=True)
    piece = jnp.sum(partial, 0)
    pieces = [rows_to_block(piece, d) for d in range(NX)]

    retain = jnp.exp(-decay_rate)
    powers, total = local(
        power_kernel, "powers", [],
        infos + [decay_rate[None, :], jnp.broadcast_to(retain[:, None], (modes, modes))],
        [f32(LEVELS, modes, modes), square], 8 * 6 * 2 * modes**3, tokens=[done],
    )
    steps = LEVELS // 2
    adding, spreading = local(
        factor_kernel, "factors", [], [powers],
        [
            jax.ShapeDtypeStruct((steps, 9 * modes, modes), jnp.bfloat16),
            jax.ShapeDtypeStruct((steps, 3 * modes, 3 * modes), jnp.bfloat16),
        ],
        4 * 6 * 2 * modes**3,
    )
    drive, tail = local(
        tail_kernel, "tail", [place], pieces + [decay_rate[None, :], prior_mean[None, :], adding, spreading],
        [f32(STEPS, modes), f32(8, modes)], 8 * 6 * 2 * modes**3,
    )
    terms = jax.ShapeDtypeStruct((3 * modes, modes), jnp.bfloat16)
    got = lax.ppermute(total, "c", [(0, 1), (1, 0)])
    total, lead, rest, *pair_terms = local(
        pair_kernel, "pairs", [place], [total, got], [square] * 3 + [terms] * 2, 6 * 2 * modes**3
    )
    leads, rests = [pair_terms[0]], [pair_terms[1]]
    for axis, size, bits, tokens in (("y", NY, y, []), ("z", NZ, z, [tail])):
        got = [lax.ppermute(total, axis, [(i, i ^ d) for i in range(size)]) for d in (1, 2, 3)]
        total, lead, rest, *quad_terms = local(
            quad_kernel, "quads_" + axis, [bits.astype(jnp.int32)[None]], [total] + got + [lead, rest],
            [square] * 3 + [terms] * 4, 5 * 6 * 2 * modes**3, tokens=tokens,
        )
        leads += quad_terms[::2]
        rests += quad_terms[1::2]

    (sends,) = local(
        send_kernel, "sends", [place], [tail] + rests, [f32(NK, modes)], 5 * 6 * 2 * modes**3
    )
    offsets = lax.all_to_all(sends, ("z", "y", "c"), split_axis=0, concat_axis=0, tiled=True)
    (swept,) = local(
        sweep_kernel, "sweep", [], [drive, spreading], [f32(STEPS, modes)], 8 * 12 * 2 * modes**3
    )
    (states,) = local(
        state_kernel, "states", [place], [offsets, spreading, swept] + leads,
        [f32(STEPS, modes)], 15 * 6 * 2 * modes**3,
    )
    return states


def solution(mesh):
    fine = Mesh(mesh.devices.reshape(NZ, NY, NC, NX), ("z", "y", "c", "x"))
    return jax.shard_map(
        on_device,
        mesh=fine,
        in_specs=(
            P(("x", "z", "y", "c"), None),
            P("x", None),
            P("x", None, None),
            P(("z", "y", "c"), "x"),
            P(),
            P(),
        ),
        out_specs=P(("z", "y", "c"), None),
        check_vma=False,
    )
```

```python
import jax
import jax.numpy as jnp
from jax import lax
from jax.experimental import pallas as pl
from jax.experimental.pallas import tpu as pltpu
from jax.sharding import Mesh, PartitionSpec as P

NZ, NY, NC, NX = 8, 4, 2, 4
NK = NZ * NY * NC
STEPS = 256
LEVELS = 8
SCAN = 6
LANES = 128
TAKERS = NY * NC * 2
HIGHEST = lax.Precision.HIGHEST
WHOLE = pl.BlockSpec(memory_space=pltpu.VMEM)
SCALARS = pl.BlockSpec(memory_space=pltpu.SMEM)


def dot(a, b):
    return jnp.dot(a, b, precision=HIGHEST, preferred_element_type=jnp.float32)


def f32(*shape):
    return jax.ShapeDtypeStruct(shape, jnp.float32)


def local(body, name, scalars, arrays, outs, flops, tokens=(), scratch=(), moved=1 << 20):
    inputs = len(scalars) + len(arrays)

    def call(*refs):
        body(*refs[:inputs], *refs[inputs + len(tokens) :])

    return pl.pallas_call(
        call,
        name=name,
        out_shape=outs,
        in_specs=[SCALARS] * len(scalars)
        + [WHOLE] * (len(arrays) + len(tokens)),
        out_specs=[WHOLE] * len(outs),
        scratch_shapes=list(scratch),
        cost_estimate=pl.CostEstimate(flops=flops, bytes_accessed=moved, transcendentals=0),
        compiler_params=pltpu.CompilerParams(vmem_limit_bytes=32 << 20),
    )(*scalars, *arrays, *tokens)


def split(a):
    high = a.astype(jnp.bfloat16)
    return high, (a - high.astype(jnp.float32)).astype(jnp.bfloat16)


def wide(a):
    high, low = split(a)
    return jnp.concatenate([high, low, high], 1)


def tall(a):
    high, low = split(a)
    return jnp.concatenate([high, high, low], 0)


def times(terms, factor):
    return jnp.dot(terms, factor, preferred_element_type=jnp.float32)


def xor_over_x(block, distance):
    return lax.ppermute(block, "x", [(i, i ^ distance) for i in range(NX)])


def rows_to_block(piece, distance):
    route = []
    for z in range(NZ):
        for x in range(NX):
            part = 2 * (x // 2) + z % 2
            route.append((z * NX + x, (z // 2 * 2 + x % 2) * NX + (part ^ distance)))
    return lax.ppermute(piece, ("z", "x"), route)


def order_kernel(rows_ref, out_ref):
    for m in range(NZ // 2):
        for par in range(2):
            for j in range(TAKERS):
                lane = ((m * 2 + par) * TAKERS + j) * LANES
                out_ref[j, par, m] = rows_ref[:, lane : lane + LANES]


def by_taker(observations):
    rows = observations.shape[0]
    out = pl.pallas_call(
        order_kernel,
        name="by_taker",
        out_shape=jax.ShapeDtypeStruct((TAKERS, 2, NZ // 2, rows, LANES), jnp.bfloat16),
        in_specs=[WHOLE],
        out_specs=WHOLE,
        cost_estimate=pl.CostEstimate(flops=0, bytes_accessed=4 << 20, transcendentals=0),
        compiler_params=pltpu.CompilerParams(vmem_limit_bytes=32 << 20),
    )(observations)
    return out.reshape(TAKERS * 2, NZ // 2 * rows, LANES)


def pack_kernel(kept_ref, noise_ref, map_ref, out_ref, noise_held, map_held, sems):
    first = lax.axis_index("z") * NY + lax.axis_index("c") * 2
    copies = [
        pltpu.make_async_copy(noise_ref.at[pl.ds(first, 2)], noise_held, sems.at[0]),
        pltpu.make_async_copy(map_ref.at[pl.ds(first * LANES, 2 * LANES)], map_held, sems.at[1]),
    ]
    for copy in copies:
        copy.start()
    blocks = kept_ref.shape[1]
    lane = lax.broadcasted_iota(jnp.int32, (16, LANES), 1) - lax.axis_index("x") * blocks
    row = jnp.zeros((16, LANES), jnp.float32)
    for b in range(blocks):
        row = jnp.where(lane == b, kept_ref[0, b].astype(jnp.float32), row)
    out_ref[LANES:, :LANES] = row.astype(jnp.bfloat16)
    out_ref[LANES:, LANES:] = jnp.zeros((16, LANES), jnp.bfloat16)
    for copy in copies:
        copy.wait()
    for b in range(2):
        weights = jnp.dot(
            noise_held[b], map_held[b * LANES : (b + 1) * LANES, :], preferred_element_type=jnp.float32
        )
        out_ref[:LANES, b * LANES : (b + 1) * LANES] = weights.T.astype(jnp.bfloat16)


def pack(availability, noise_precision, sensor_map):
    return pl.pallas_call(
        pack_kernel,
        name="pack",
        out_shape=jax.ShapeDtypeStruct((LANES + 16, 2 * LANES), jnp.bfloat16),
        in_specs=[SCALARS, pl.BlockSpec(memory_space=pl.ANY), pl.BlockSpec(memory_space=pl.ANY)],
        out_specs=WHOLE,
        scratch_shapes=[
            pltpu.VMEM((2, LANES, LANES), jnp.bfloat16),
            pltpu.VMEM((2 * LANES, LANES), jnp.bfloat16),
            pltpu.SemaphoreType.DMA((2,)),
        ],
        cost_estimate=pl.CostEstimate(flops=1 << 23, bytes_accessed=1 << 18, transcendentals=0),
    )(availability, noise_precision, sensor_map)


def gather_kernel(place_ref, own_ref, one_ref, two_ref, three_ref, kept_ref, half_ref, held_ref, sems):
    copies = [
        pltpu.make_async_copy(ref, held_ref.at[r], sems.at[r])
        for r, ref in enumerate((own_ref, one_ref, two_ref, three_ref))
    ]
    for copy in copies:
        copy.start()
    for copy in copies:
        copy.wait()
    kept = sum(held_ref[r, LANES:, :LANES].astype(jnp.float32)[:NZ] for r in range(NX))
    at = lax.broadcasted_iota(jnp.int32, (NZ, LANES), 0)
    kept_ref[...] = jnp.where(at == place_ref[2], kept, 0.0)
    for r in range(NX):
        half_ref[:, 2 * r * LANES : 2 * (r + 1) * LANES] = held_ref[r, :LANES]


def gather(place, packets):
    return pl.pallas_call(
        gather_kernel,
        name="gather",
        out_shape=[f32(NZ, LANES), jax.ShapeDtypeStruct((LANES, NX * 2 * LANES), jnp.bfloat16)],
        in_specs=[SCALARS] + [pl.BlockSpec(memory_space=pl.ANY)] * NX,
        out_specs=[WHOLE] * 2,
        scratch_shapes=[
            pltpu.VMEM((NX,) + packets[0].shape, jnp.bfloat16),
            pltpu.SemaphoreType.DMA((NX,)),
        ],
        cost_estimate=pl.CostEstimate(flops=0, bytes_accessed=1 << 20, transcendentals=0),
    )(place, *packets)


def weigh_kernel(kept_ref, noise_ref, map_ref, out_ref):
    step = pl.program_id(0)
    blocks, sblk = noise_ref.shape[0], noise_ref.shape[1]
    parts = []
    for b in range(blocks):
        weights = jnp.dot(
            noise_ref[b], map_ref[b * sblk : (b + 1) * sblk, :], preferred_element_type=jnp.float32
        )
        parts.append((weights * kept_ref[0, step * blocks + b].astype(jnp.float32)).astype(jnp.bfloat16))
    share = lax.dot_general(
        jnp.concatenate(parts, 0), map_ref[...], (((0,), (0,)), ((), ())), preferred_element_type=jnp.float32
    )

    @pl.when(step == 0)
    def _():
        out_ref[...] = share

    @pl.when(step > 0)
    def _():
        out_ref[...] += share


def weigh(availability, noise_precision, sensor_map):
    blocks, sblk, _ = noise_precision.shape
    step = blocks // 4
    return pl.pallas_call(
        weigh_kernel,
        name="weigh",
        grid=(4,),
        out_shape=f32(LANES, LANES),
        in_specs=[
            SCALARS,
            pl.BlockSpec((step, sblk, sblk), lambda i: (i, 0, 0)),
            pl.BlockSpec((step * sblk, LANES), lambda i: (i, 0)),
        ],
        out_specs=pl.BlockSpec((LANES, LANES), lambda i: (0, 0)),
        cost_estimate=pl.CostEstimate(flops=4 * blocks * sblk**3, bytes_accessed=2 << 20, transcendentals=0),
    )(availability, noise_precision, sensor_map)


def power_kernel(own_ref, one_ref, two_ref, three_ref, decay_ref, retain_ref, out_ref, block_ref):
    info = (own_ref[...] + one_ref[...]) + (two_ref[...] + three_ref[...])
    row = lax.broadcasted_iota(jnp.int32, info.shape, 0)
    column = lax.broadcasted_iota(jnp.int32, info.shape, 1)
    identity = jnp.where(row == column, 1.0, 0.0)
    power = (identity - decay_ref[...] * info) * retain_ref[...]
    for level in range(LEVELS):
        out_ref[level] = power
        power = dot(power, power)
    block_ref[...] = power


def factor_kernel(power_ref, add_ref, spread_ref):
    for step in range(LEVELS // 2):
        one, two = power_ref[2 * step], power_ref[2 * step + 1]
        for j, power in enumerate((one, two, dot(one, two))):
            terms = tall(power)
            add_ref[step, (2 - j) * 3 * LANES : (3 - j) * 3 * LANES] = terms
            spread_ref[step, :, j * LANES : (j + 1) * LANES] = terms


def once_kernel(array_ref, *refs):
    pass


def once(array, *tokens):
    return pl.pallas_call(
        once_kernel,
        name="once",
        out_shape=jax.ShapeDtypeStruct(array.shape, array.dtype),
        in_specs=[pl.BlockSpec(memory_space=pl.ANY)] * (1 + len(tokens)),
        out_specs=pl.BlockSpec(memory_space=pl.ANY),
        input_output_aliases={0: 0},
        compiler_params=pltpu.CompilerParams(vmem_limit_bytes=60 << 20),
    )(array, *tokens)


def factor_kernel(power_ref, add_ref, spread_ref):
    for step in range(LEVELS // 2):
        one, two = power_ref[2 * step], power_ref[2 * step + 1]
        for j, power in enumerate((one, two, dot(one, two))):
            terms = tall(power)
            add_ref[step, (2 - j) * 3 * LANES : (3 - j) * 3 * LANES] = terms
            spread_ref[step, :, j * LANES : (j + 1) * LANES] = terms


def joined(upper, total, beside, lead, rest):
    both = dot(jnp.where(upper, beside, total), jnp.where(upper, total, beside))
    new = dot(jnp.where(upper, beside, rest), jnp.where(upper, lead, beside))
    return both, jnp.where(upper, new, lead), jnp.where(upper, rest, new)


def pair_kernel(place_ref, total_ref, got_ref, total_out, lead_out, rest_out, lead_terms, rest_terms):
    row = lax.broadcasted_iota(jnp.int32, (LANES, LANES), 0)
    column = lax.broadcasted_iota(jnp.int32, (LANES, LANES), 1)
    identity = jnp.where(row == column, 1.0, 0.0)
    upper = place_ref[1] % 2 == 1
    total, got = total_ref[...], got_ref[...]
    lead, rest = jnp.where(upper, got, identity), jnp.where(upper, identity, got)
    total_out[...] = dot(jnp.where(upper, got, total), jnp.where(upper, total, got))
    lead_out[...], rest_out[...] = lead, rest
    lead_terms[...], rest_terms[...] = tall(lead), tall(rest)


def quad_kernel(bits_ref, total_ref, one_ref, two_ref, three_ref, lead_ref, rest_ref, total_out, lead_out, rest_out, *terms):
    odd, upper = bits_ref[0] % 2 == 1, bits_ref[0] % 4 >= 2
    two, three = two_ref[...], three_ref[...]
    total, lead, rest = joined(odd, total_ref[...], one_ref[...], lead_ref[...], rest_ref[...])
    terms[0][...], terms[1][...] = tall(lead), tall(rest)
    beside = dot(jnp.where(odd, three, two), jnp.where(odd, two, three))
    total, lead, rest = joined(upper, total, beside, lead, rest)
    terms[2][...], terms[3][...] = tall(lead), tall(rest)
    total_out[...], lead_out[...], rest_out[...] = total, lead, rest


def mask_kernel(place_ref, kept_ref, own_ref, other_ref, plane_ref, mask_ref):
    x, z, c = place_ref[0], place_ref[2], place_ref[3]
    half = NZ // 2
    zs = lax.broadcasted_iota(jnp.int32, (NZ, NZ), 1)
    pick = lax.broadcasted_iota(jnp.int32, (NZ, NZ), 0) * 2 + x % 2
    kept = jnp.dot(
        jnp.where(zs == pick, 1.0, 0.0).astype(jnp.bfloat16),
        kept_ref[...].astype(jnp.bfloat16),
        preferred_element_type=jnp.float32,
    ).astype(jnp.bfloat16)
    width = NY * LANES
    block = lax.broadcasted_iota(jnp.int32, (LANES, width), 0)
    lane = lax.broadcasted_iota(jnp.int32, (LANES, width), 1) // LANES
    for r in range(NX):
        own, other = own_ref[:, r * width // 2 : (r + 1) * width // 2], other_ref[:, r * width // 2 : (r + 1) * width // 2]
        plane_ref[:, r * width : r * width + width // 2] = jnp.where(c == 0, own, other)
        plane_ref[:, r * width + width // 2 : (r + 1) * width] = jnp.where(c == 0, other, own)
        spread = jnp.where(block == (x ^ r) * (NZ * NY) + z * NY + lane, 1.0, 0.0).astype(jnp.bfloat16)
        mask_ref[:, r * width : (r + 1) * width] = jnp.dot(kept, spread, preferred_element_type=jnp.float32)


def rows_kernel(place_ref, mask_ref, plane_ref, got_ref, out_ref, token_ref, held_ref, sems):
    token_ref[...] = jnp.zeros((8, LANES), jnp.float32)
    x = place_ref[0]
    width = NY * LANES
    copies = [
        pltpu.make_async_copy(got_ref.at[:, :, m], held_ref.at[m], sems.at[m]) for m in range(NZ // 2)
    ]
    for copy in copies:
        copy.start()
    for m, copy in enumerate(copies):
        copy.wait()
        mask = mask_ref[m : m + 1, :].astype(jnp.bfloat16)
        weights = plane_ref[...] * mask
        readings = jnp.concatenate([held_ref[m, :, x ^ r].reshape(width, LANES) for r in range(NX)], 0)
        out_ref[m] = jnp.dot(weights, readings, preferred_element_type=jnp.float32).T


def info_rows(place, masks, plane, received):
    takers, _, steps, rows, _ = received.shape
    return pl.pallas_call(
        rows_kernel,
        name="rows",
        out_shape=[f32(steps, LANES, LANES), f32(8, LANES)],
        in_specs=[SCALARS, WHOLE, WHOLE, pl.BlockSpec(memory_space=pl.ANY)],
        out_specs=[WHOLE] * 2,
        scratch_shapes=[
            pltpu.VMEM((steps, takers, NX, rows, LANES), jnp.bfloat16),
            pltpu.SemaphoreType.DMA((steps,)),
        ],
        cost_estimate=pl.CostEstimate(flops=1 << 28, bytes_accessed=3 << 20, transcendentals=0),
        compiler_params=pltpu.CompilerParams(vmem_limit_bytes=32 << 20),
    )(place, masks, plane, received)


def tail_kernel(place_ref, a_ref, b_ref, c_ref, d_ref, decay_ref, prior_ref, add_ref, spread_ref, *refs):
    rest_refs, (drive_ref, tail_ref, near_ref) = refs[:3], refs[3:]
    x = place_ref[0]
    rows = a_ref.shape[0]
    for r, ref in enumerate((a_ref, b_ref, c_ref, d_ref)):
        drive_ref[pl.ds(pl.multiple_of((x ^ r) * rows, rows), rows), :] = ref[...] * decay_ref[...]
    pushed = times(wide(prior_ref[...]), spread_ref[0, :, :LANES])
    drive_ref[:1] += jnp.where(place_ref[1] == 0, pushed, 0.0)
    tail = drive_ref[...]
    for step in reversed(range(LEVELS // 2)):
        n = 4**step
        terms = jnp.concatenate([wide(tail[j * n : (j + 1) * n]) for j in range(3)], 1)
        tail = times(terms, add_ref[step]) + tail[3 * n :]
    tail_ref[...] = jnp.broadcast_to(tail, (8, LANES))
    near_ref[...] = onward(place_ref[1], tail, jnp.broadcast_to(tail, (NK, LANES)), 1, [ref[...] for ref in rest_refs])


def onward(k, tail, sends, level, factors):
    to = lax.broadcasted_iota(jnp.int32, (NK, LANES), 0) ^ k
    terms = wide(tail)
    for step, factor in enumerate(factors):
        sends = jnp.where(to >= 2 ** (level + step), times(terms, factor), sends)
    return sends


def far_kernel(place_ref, total_ref, one_ref, two_ref, three_ref, lead_ref, rest_ref, tail_ref, near_ref, four_ref, five_ref, send_ref):
    odd, upper = place_ref[2] % 2 == 1, place_ref[2] % 4 >= 2
    two, three = two_ref[...], three_ref[...]
    total, lead, rest = joined(odd, total_ref[...], one_ref[...], lead_ref[...], rest_ref[...])
    four_ref[...] = tall(lead)
    factors = [tall(rest)]
    beside = dot(jnp.where(odd, three, two), jnp.where(odd, two, three))
    total, lead, rest = joined(upper, total, beside, lead, rest)
    five_ref[...] = tall(lead)
    factors.append(tall(rest))
    send_ref[...] = onward(place_ref[1], tail_ref[:1], near_ref[...], 4, factors)


def sweep_kernel(drive_ref, spread_ref, out_ref):
    swept = drive_ref[...]
    row = lax.broadcasted_iota(jnp.int32, (STEPS, LANES), 0)
    for step in range(LEVELS // 2):
        for side in range(2):
            shift = 4**step * (1 + side)
            before = jnp.where(row >= shift, pltpu.roll(swept, shift, 0), 0.0)
            swept += times(wide(before), spread_ref[step, :, side * LANES : (side + 1) * LANES])
    out_ref[...] = swept


def state_kernel(place_ref, offsets_ref, spread_ref, swept_ref, *refs):
    lead_refs, out_ref = refs[:-1], refs[-1]
    k = place_ref[1]
    index = lax.broadcasted_iota(jnp.int32, (NK, LANES), 0)
    apart = jnp.where(index < k, index ^ k, 0)
    offsets = offsets_ref[...]
    parts = []
    for level in range(SCAN):
        chosen = (apart >= 2**level) & (apart < 2 ** (level + 1))
        parts.append(jnp.sum(jnp.where(chosen, offsets, 0.0), 0, keepdims=True))
    entry = parts[0]
    for level in range(1, SCAN):
        entry += times(wide(parts[level]), lead_refs[level - 1][...])
    grown = times(wide(entry), spread_ref[0, :, :LANES])
    for step in range(LEVELS // 2):
        more = times(wide(grown), spread_ref[step])
        grown = jnp.concatenate([grown] + [more[:, j * LANES : (j + 1) * LANES] for j in range(3)], 0)
    out_ref[...] = swept_ref[...] + grown


def on_device(observations, sensor_map, noise_precision, availability, decay_rate, prior_mean):
    modes = sensor_map.shape[1]
    rows = observations.shape[0]
    z, y, c, x = (lax.axis_index(a) for a in "zycx")
    k = (z * NY + y) * NC + c
    place = jnp.stack([x, k, z, c, y]).astype(jnp.int32)
    square = f32(modes, modes)
    packet = pack(availability, noise_precision, sensor_map)
    packets = [packet] + [xor_over_x(packet, d) for d in (1, 2, 3)]
    kept, half = gather(place, packets)
    sent = once(by_taker(observations), *packets[1:])
    received = lax.all_to_all(sent, ("y", "c", "x"), split_axis=0, concat_axis=0, tiled=True)

    for flip in (1, 2, 4):
        kept = kept + lax.ppermute(kept, "z", [(i, i ^ flip) for i in range(NZ)])
    plane, masks = local(
        mask_kernel, "masks", [place], [kept, half, lax.ppermute(half, "c", [(0, 1), (1, 0)])],
        [jax.ShapeDtypeStruct((modes, NX * NY * modes), jnp.bfloat16), f32(NZ, NX * NY * modes)], 1 << 20,
    )

    info = weigh(availability, noise_precision, sensor_map)
    infos = [info] + [xor_over_x(info, d) for d in (1, 2, 3)]

    partial, done = info_rows(place, masks, plane, received.reshape(NY * NC, NX, NZ // 2, rows, LANES))
    partial = lax.all_to_all(partial.reshape(NZ, -1, modes), "z", split_axis=0, concat_axis=0, tiled=True)
    piece = jnp.sum(partial, 0)
    pieces = [rows_to_block(piece, d) for d in range(NX)]

    retain = jnp.exp(-decay_rate)
    powers, total = local(
        power_kernel, "powers", [],
        infos + [decay_rate[None, :], jnp.broadcast_to(retain[:, None], (modes, modes))],
        [f32(LEVELS, modes, modes), square], 4 * 10**10, tokens=[done],
    )
    steps = LEVELS // 2
    adding, spreading = local(
        factor_kernel, "factors", [], [powers],
        [
            jax.ShapeDtypeStruct((steps, 9 * modes, modes), jnp.bfloat16),
            jax.ShapeDtypeStruct((steps, 3 * modes, 3 * modes), jnp.bfloat16),
        ],
        4 * 6 * 2 * modes**3,
    )
    terms = jax.ShapeDtypeStruct((3 * modes, modes), jnp.bfloat16)
    got = lax.ppermute(total, "c", [(0, 1), (1, 0)])
    total, lead, rest, *pair_terms = local(
        pair_kernel, "pairs", [place], [total, got], [square] * 3 + [terms] * 2, 6 * 2 * modes**3
    )
    leads, rests = [pair_terms[0]], [pair_terms[1]]
    got = [lax.ppermute(total, "y", [(i, i ^ d) for i in range(NY)]) for d in (1, 2, 3)]
    total, lead, rest, *quad_terms = local(
        quad_kernel, "quads", [y.astype(jnp.int32)[None]], [total] + got + [lead, rest],
        [square] * 3 + [terms] * 4, 5 * 6 * 2 * modes**3,
    )
    leads += quad_terms[::2]
    rests += quad_terms[1::2]
    got = [lax.ppermute(total, "z", [(i, i ^ d) for i in range(NZ)]) for d in (1, 2, 3)]

    drive, tail, near = local(
        tail_kernel, "tail", [place],
        pieces + [decay_rate[None, :], prior_mean[None, :], adding, spreading] + rests,
        [f32(STEPS, modes), f32(8, modes), f32(NK, modes)], 8 * 6 * 2 * modes**3,
    )
    *far_terms, sends = local(
        far_kernel, "far", [place], [total] + got + [lead, rest, tail, near],
        [terms] * 2 + [f32(NK, modes)], 5 * 6 * 2 * modes**3,
    )
    leads += far_terms

    offsets = lax.all_to_all(sends, ("z", "y", "c"), split_axis=0, concat_axis=0, tiled=True)
    (swept,) = local(
        sweep_kernel, "sweep", [], [drive, spreading], [f32(STEPS, modes)], 8 * 12 * 2 * modes**3
    )
    (states,) = local(
        state_kernel, "states", [place], [offsets, spreading, swept] + leads,
        [f32(STEPS, modes)], 15 * 6 * 2 * modes**3,
    )
    return states


def solution(mesh):
    fine = Mesh(mesh.devices.reshape(NZ, NY, NC, NX), ("z", "y", "c", "x"))
    return jax.shard_map(
        on_device,
        mesh=fine,
        in_specs=(
            P(("x", "z", "y", "c"), None),
            P("x", None),
            P("x", None, None),
            P(("z", "y", "c"), "x"),
            P(),
            P(),
        ),
        out_specs=P(("z", "y", "c"), None),
        check_vma=False,
    )
```

```python
import jax
import jax.numpy as jnp
from jax import lax
from jax.experimental import pallas as pl
from jax.experimental.pallas import tpu as pltpu
from jax.sharding import Mesh, PartitionSpec as P

NZ, NY, NC, NX = 8, 4, 2, 4
NK = NZ * NY * NC
STEPS = 256
LEVELS = 8
SCAN = 6
LANES = 128
HIGHEST = lax.Precision.HIGHEST
WHOLE = pl.BlockSpec(memory_space=pltpu.VMEM)
SCALARS = pl.BlockSpec(memory_space=pltpu.SMEM)


def dot(a, b):
    return jnp.dot(a, b, precision=HIGHEST, preferred_element_type=jnp.float32)


def f32(*shape):
    return jax.ShapeDtypeStruct(shape, jnp.float32)


def local(body, name, scalars, arrays, outs, flops, tokens=(), scratch=(), moved=1 << 20):
    inputs = len(scalars) + len(arrays)

    def call(*refs):
        body(*refs[:inputs], *refs[inputs + len(tokens) :])

    return pl.pallas_call(
        call,
        name=name,
        out_shape=outs,
        in_specs=[SCALARS] * len(scalars)
        + [WHOLE] * (len(arrays) + len(tokens)),
        out_specs=[WHOLE] * len(outs),
        scratch_shapes=list(scratch),
        cost_estimate=pl.CostEstimate(flops=flops, bytes_accessed=moved, transcendentals=0),
        compiler_params=pltpu.CompilerParams(vmem_limit_bytes=32 << 20),
    )(*scalars, *arrays, *tokens)


def split(a):
    high = a.astype(jnp.bfloat16)
    return high, (a - high.astype(jnp.float32)).astype(jnp.bfloat16)


def wide(a):
    high, low = split(a)
    return jnp.concatenate([high, low, high], 1)


def tall(a):
    high, low = split(a)
    return jnp.concatenate([high, high, low], 0)


def times(terms, factor):
    return jnp.dot(terms, factor, preferred_element_type=jnp.float32)


def xor_over_x(block, distance):
    return lax.ppermute(block, "x", [(i, i ^ distance) for i in range(NX)])


def order_kernel(rows_ref, out_ref):
    half, side = rows_ref.shape[0] // 2, LANES // 2
    for k in range(NZ):
        for j in range(NY * NC):
            for pair in range(2):
                lane = ((k * NY * NC + j) * 2 + pair) * LANES
                upper = rows_ref[:half, lane : lane + LANES]
                lower = rows_ref[half:, lane : lane + LANES]
                out_ref[j, 2 * pair, k] = jnp.concatenate([upper[:, :side], lower[:, :side]], 1)
                out_ref[j, 2 * pair + 1, k] = jnp.concatenate([upper[:, side:], lower[:, side:]], 1)


def by_taker(observations):
    half = observations.shape[0] // 2
    out = pl.pallas_call(
        order_kernel,
        name="by_taker",
        out_shape=jax.ShapeDtypeStruct((NY * NC, NX, NZ, half, LANES), jnp.bfloat16),
        in_specs=[WHOLE],
        out_specs=WHOLE,
        cost_estimate=pl.CostEstimate(flops=0, bytes_accessed=4 << 20, transcendentals=0),
        compiler_params=pltpu.CompilerParams(vmem_limit_bytes=32 << 20),
    )(observations)
    return out.reshape(NY * NC * NX, NZ * half, LANES)


def pack_kernel(kept_ref, noise_ref, map_ref, out_ref, noise_held, map_held, sems):
    first = lax.axis_index("z") * NY + lax.axis_index("c") * 2
    copies = [
        pltpu.make_async_copy(noise_ref.at[pl.ds(first, 2)], noise_held, sems.at[0]),
        pltpu.make_async_copy(map_ref.at[pl.ds(first * LANES, 2 * LANES)], map_held, sems.at[1]),
    ]
    for copy in copies:
        copy.start()
    blocks = kept_ref.shape[1]
    lane = lax.broadcasted_iota(jnp.int32, (16, LANES), 1) - lax.axis_index("x") * blocks
    row = jnp.zeros((16, LANES), jnp.float32)
    for b in range(blocks):
        row = jnp.where(lane == b, kept_ref[0, b].astype(jnp.float32), row)
    out_ref[LANES:, :LANES] = row.astype(jnp.bfloat16)
    out_ref[LANES:, LANES:] = jnp.zeros((16, LANES), jnp.bfloat16)
    for copy in copies:
        copy.wait()
    for b in range(2):
        weights = jnp.dot(
            noise_held[b], map_held[b * LANES : (b + 1) * LANES, :], preferred_element_type=jnp.float32
        )
        out_ref[:LANES, b * LANES : (b + 1) * LANES] = weights.T.astype(jnp.bfloat16)


def pack(availability, noise_precision, sensor_map):
    return pl.pallas_call(
        pack_kernel,
        name="pack",
        out_shape=jax.ShapeDtypeStruct((LANES + 16, 2 * LANES), jnp.bfloat16),
        in_specs=[SCALARS, pl.BlockSpec(memory_space=pl.ANY), pl.BlockSpec(memory_space=pl.ANY)],
        out_specs=WHOLE,
        scratch_shapes=[
            pltpu.VMEM((2, LANES, LANES), jnp.bfloat16),
            pltpu.VMEM((2 * LANES, LANES), jnp.bfloat16),
            pltpu.SemaphoreType.DMA((2,)),
        ],
        cost_estimate=pl.CostEstimate(flops=1 << 23, bytes_accessed=1 << 18, transcendentals=0),
    )(availability, noise_precision, sensor_map)


def gather_kernel(place_ref, own_ref, one_ref, two_ref, three_ref, kept_ref, half_ref, held_ref, sems):
    copies = [
        pltpu.make_async_copy(ref, held_ref.at[r], sems.at[r])
        for r, ref in enumerate((own_ref, one_ref, two_ref, three_ref))
    ]
    for copy in copies:
        copy.start()
    for copy in copies:
        copy.wait()
    kept = sum(held_ref[r, LANES:, :LANES].astype(jnp.float32)[:NZ] for r in range(NX))
    at = lax.broadcasted_iota(jnp.int32, (NZ, LANES), 0)
    kept_ref[...] = jnp.where(at == place_ref[2], kept, 0.0)
    for r in range(NX):
        half_ref[:, 2 * r * LANES : 2 * (r + 1) * LANES] = held_ref[r, :LANES]


def gather(place, packets):
    return pl.pallas_call(
        gather_kernel,
        name="gather",
        out_shape=[f32(NZ, LANES), jax.ShapeDtypeStruct((LANES, NX * 2 * LANES), jnp.bfloat16)],
        in_specs=[SCALARS] + [pl.BlockSpec(memory_space=pl.ANY)] * NX,
        out_specs=[WHOLE] * 2,
        scratch_shapes=[
            pltpu.VMEM((NX,) + packets[0].shape, jnp.bfloat16),
            pltpu.SemaphoreType.DMA((NX,)),
        ],
        cost_estimate=pl.CostEstimate(flops=0, bytes_accessed=1 << 20, transcendentals=0),
    )(place, *packets)


def weigh_kernel(kept_ref, noise_ref, map_ref, out_ref):
    step = pl.program_id(0)
    blocks, sblk = noise_ref.shape[0], noise_ref.shape[1]
    parts = []
    for b in range(blocks):
        weights = jnp.dot(
            noise_ref[b], map_ref[b * sblk : (b + 1) * sblk, :], preferred_element_type=jnp.float32
        )
        parts.append((weights * kept_ref[0, step * blocks + b].astype(jnp.float32)).astype(jnp.bfloat16))
    share = lax.dot_general(
        jnp.concatenate(parts, 0), map_ref[...], (((0,), (0,)), ((), ())), preferred_element_type=jnp.float32
    )

    @pl.when(step == 0)
    def _():
        out_ref[...] = share

    @pl.when(step > 0)
    def _():
        out_ref[...] += share


def weigh(availability, noise_precision, sensor_map):
    blocks, sblk, _ = noise_precision.shape
    step = blocks // 4
    return pl.pallas_call(
        weigh_kernel,
        name="weigh",
        grid=(4,),
        out_shape=f32(LANES, LANES),
        in_specs=[
            SCALARS,
            pl.BlockSpec((step, sblk, sblk), lambda i: (i, 0, 0)),
            pl.BlockSpec((step * sblk, LANES), lambda i: (i, 0)),
        ],
        out_specs=pl.BlockSpec((LANES, LANES), lambda i: (0, 0)),
        cost_estimate=pl.CostEstimate(flops=4 * blocks * sblk**3, bytes_accessed=2 << 20, transcendentals=0),
    )(availability, noise_precision, sensor_map)


def power_kernel(own_ref, one_ref, two_ref, three_ref, decay_ref, retain_ref, out_ref, block_ref):
    info = (own_ref[...] + one_ref[...]) + (two_ref[...] + three_ref[...])
    row = lax.broadcasted_iota(jnp.int32, info.shape, 0)
    column = lax.broadcasted_iota(jnp.int32, info.shape, 1)
    identity = jnp.where(row == column, 1.0, 0.0)
    power = (identity - decay_ref[...] * info) * retain_ref[...]
    for level in range(LEVELS):
        out_ref[level] = power
        power = dot(power, power)
    block_ref[...] = power


def factor_kernel(power_ref, add_ref, spread_ref):
    for step in range(LEVELS // 2):
        one, two = power_ref[2 * step], power_ref[2 * step + 1]
        for j, power in enumerate((one, two, dot(one, two))):
            terms = tall(power)
            add_ref[step, (2 - j) * 3 * LANES : (3 - j) * 3 * LANES] = terms
            spread_ref[step, :, j * LANES : (j + 1) * LANES] = terms


def once_kernel(array_ref, *refs):
    pass


def once(array, *tokens):
    return pl.pallas_call(
        once_kernel,
        name="once",
        out_shape=jax.ShapeDtypeStruct(array.shape, array.dtype),
        in_specs=[pl.BlockSpec(memory_space=pl.ANY)] * (1 + len(tokens)),
        out_specs=pl.BlockSpec(memory_space=pl.ANY),
        input_output_aliases={0: 0},
        compiler_params=pltpu.CompilerParams(vmem_limit_bytes=60 << 20),
    )(array, *tokens)


def factor_kernel(power_ref, add_ref, spread_ref):
    for step in range(LEVELS // 2):
        one, two = power_ref[2 * step], power_ref[2 * step + 1]
        for j, power in enumerate((one, two, dot(one, two))):
            terms = tall(power)
            add_ref[step, (2 - j) * 3 * LANES : (3 - j) * 3 * LANES] = terms
            spread_ref[step, :, j * LANES : (j + 1) * LANES] = terms


def joined(upper, total, beside, lead, rest):
    both = dot(jnp.where(upper, beside, total), jnp.where(upper, total, beside))
    new = dot(jnp.where(upper, beside, rest), jnp.where(upper, lead, beside))
    return both, jnp.where(upper, new, lead), jnp.where(upper, rest, new)


def pair_kernel(place_ref, total_ref, got_ref, total_out, lead_out, rest_out, lead_terms, rest_terms):
    row = lax.broadcasted_iota(jnp.int32, (LANES, LANES), 0)
    column = lax.broadcasted_iota(jnp.int32, (LANES, LANES), 1)
    identity = jnp.where(row == column, 1.0, 0.0)
    upper = place_ref[1] % 2 == 1
    total, got = total_ref[...], got_ref[...]
    lead, rest = jnp.where(upper, got, identity), jnp.where(upper, identity, got)
    total_out[...] = dot(jnp.where(upper, got, total), jnp.where(upper, total, got))
    lead_out[...], rest_out[...] = lead, rest
    lead_terms[...], rest_terms[...] = tall(lead), tall(rest)


def quad_kernel(bits_ref, total_ref, one_ref, two_ref, three_ref, lead_ref, rest_ref, total_out, lead_out, rest_out, *terms):
    odd, upper = bits_ref[0] % 2 == 1, bits_ref[0] % 4 >= 2
    two, three = two_ref[...], three_ref[...]
    total, lead, rest = joined(odd, total_ref[...], one_ref[...], lead_ref[...], rest_ref[...])
    terms[0][...], terms[1][...] = tall(lead), tall(rest)
    beside = dot(jnp.where(odd, three, two), jnp.where(odd, two, three))
    total, lead, rest = joined(upper, total, beside, lead, rest)
    terms[2][...], terms[3][...] = tall(lead), tall(rest)
    total_out[...], lead_out[...], rest_out[...] = total, lead, rest


def mask_kernel(place_ref, kept_ref, own_ref, other_ref, plane_ref, mask_ref):
    x, z, c = place_ref[0], place_ref[2], place_ref[3]
    width = NY * LANES
    kept = kept_ref[...].astype(jnp.bfloat16)
    block = lax.broadcasted_iota(jnp.int32, (LANES, width // 2), 0)
    lane = lax.broadcasted_iota(jnp.int32, (LANES, width // 2), 1) // (LANES // 2)
    source = lax.broadcasted_iota(jnp.int32, (width, width // 2), 0)
    target = lax.broadcasted_iota(jnp.int32, (width, width // 2), 1)
    picks = [
        jnp.where(source == target // 32 * 64 + target % 32 + 32 * side, 1.0, 0.0).astype(jnp.bfloat16)
        for side in range(2)
    ]
    for r in range(NX):
        lanes = slice(r * width // 2, (r + 1) * width // 2)
        own, other = own_ref[:, lanes], other_ref[:, lanes]
        whole = jnp.concatenate([jnp.where(c == 0, own, other), jnp.where(c == 0, other, own)], 1)
        for side in range(2):
            plane_ref[side * LANES : (side + 1) * LANES, lanes] = jnp.dot(
                whole, picks[side], preferred_element_type=jnp.float32
            ).astype(jnp.bfloat16)
        spread = jnp.where(block == (x ^ r) * (NZ * NY) + z * NY + lane, 1.0, 0.0).astype(jnp.bfloat16)
        mask_ref[:, lanes] = jnp.dot(kept, spread, preferred_element_type=jnp.float32)


def rows_kernel(place_ref, mask_ref, plane_ref, got_ref, out_ref, token_ref):
    x = place_ref[0]
    token_ref[...] = jnp.zeros((8, LANES), jnp.float32)
    rows = plane_ref.shape[1] // NX
    side = LANES // 2
    left = lax.broadcasted_iota(jnp.int32, (LANES, LANES), 1) < side
    for k in range(NZ):
        weights = plane_ref[...] * mask_ref[k : k + 1, :].astype(jnp.bfloat16)
        readings = jnp.concatenate([got_ref[:, x ^ r, k].reshape(rows, LANES) for r in range(NX)], 0)
        both = jnp.dot(weights, readings, preferred_element_type=jnp.float32)
        upper, lower = both[:LANES], both[LANES:]
        if k % 2 == 0:
            first = upper + pltpu.roll(lower, side, 1)
        else:
            second = lower + pltpu.roll(upper, side, 1)
            pair = jnp.where(left, first, second).T
            out_ref[k - 1], out_ref[k] = pair[:side], pair[side:]


def info_rows(place, masks, plane, received):
    return pl.pallas_call(
        rows_kernel,
        name="rows",
        out_shape=[f32(NZ, LANES // 2, LANES), f32(8, LANES)],
        in_specs=[SCALARS, WHOLE, WHOLE, WHOLE],
        out_specs=[WHOLE] * 2,
        cost_estimate=pl.CostEstimate(flops=1 << 28, bytes_accessed=3 << 20, transcendentals=0),
        compiler_params=pltpu.CompilerParams(vmem_limit_bytes=32 << 20),
    )(place, masks, plane, received)


def tail_kernel(place_ref, a_ref, b_ref, c_ref, d_ref, decay_ref, prior_ref, add_ref, spread_ref, *refs):
    rest_refs, (drive_ref, tail_ref, near_ref) = refs[:3], refs[3:]
    x = place_ref[0]
    rows = a_ref.shape[0]
    for r, ref in enumerate((a_ref, b_ref, c_ref, d_ref)):
        drive_ref[pl.ds(pl.multiple_of((x ^ r) * rows, rows), rows), :] = ref[...] * decay_ref[...]
    pushed = times(wide(prior_ref[...]), spread_ref[0, :, :LANES])
    drive_ref[:1] += jnp.where(place_ref[1] == 0, pushed, 0.0)
    tail = drive_ref[...]
    for step in reversed(range(LEVELS // 2)):
        n = 4**step
        terms = jnp.concatenate([wide(tail[j * n : (j + 1) * n]) for j in range(3)], 1)
        tail = times(terms, add_ref[step]) + tail[3 * n :]
    tail_ref[...] = jnp.broadcast_to(tail, (8, LANES))
    near_ref[...] = onward(place_ref[1], tail, jnp.broadcast_to(tail, (NK, LANES)), 1, [ref[...] for ref in rest_refs])


def onward(k, tail, sends, level, factors):
    to = lax.broadcasted_iota(jnp.int32, (NK, LANES), 0) ^ k
    terms = wide(tail)
    for step, factor in enumerate(factors):
        sends = jnp.where(to >= 2 ** (level + step), times(terms, factor), sends)
    return sends


def far_kernel(place_ref, total_ref, one_ref, two_ref, three_ref, lead_ref, rest_ref, tail_ref, near_ref, four_ref, five_ref, send_ref):
    odd, upper = place_ref[2] % 2 == 1, place_ref[2] % 4 >= 2
    two, three = two_ref[...], three_ref[...]
    total, lead, rest = joined(odd, total_ref[...], one_ref[...], lead_ref[...], rest_ref[...])
    four_ref[...] = tall(lead)
    factors = [tall(rest)]
    beside = dot(jnp.where(odd, three, two), jnp.where(odd, two, three))
    total, lead, rest = joined(upper, total, beside, lead, rest)
    five_ref[...] = tall(lead)
    factors.append(tall(rest))
    send_ref[...] = onward(place_ref[1], tail_ref[:1], near_ref[...], 4, factors)


def sweep_kernel(drive_ref, spread_ref, out_ref):
    swept = drive_ref[...]
    row = lax.broadcasted_iota(jnp.int32, (STEPS, LANES), 0)
    for step in range(LEVELS // 2):
        for side in range(2):
            shift = 4**step * (1 + side)
            before = jnp.where(row >= shift, pltpu.roll(swept, shift, 0), 0.0)
            swept += times(wide(before), spread_ref[step, :, side * LANES : (side + 1) * LANES])
    out_ref[...] = swept


def state_kernel(place_ref, offsets_ref, spread_ref, swept_ref, *refs):
    lead_refs, out_ref = refs[:-1], refs[-1]
    k = place_ref[1]
    index = lax.broadcasted_iota(jnp.int32, (NK, LANES), 0)
    apart = jnp.where(index < k, index ^ k, 0)
    offsets = offsets_ref[...]
    parts = []
    for level in range(SCAN):
        chosen = (apart >= 2**level) & (apart < 2 ** (level + 1))
        parts.append(jnp.sum(jnp.where(chosen, offsets, 0.0), 0, keepdims=True))
    entry = parts[0]
    for level in range(1, SCAN):
        entry += times(wide(parts[level]), lead_refs[level - 1][...])
    grown = times(wide(entry), spread_ref[0, :, :LANES])
    for step in range(LEVELS // 2):
        more = times(wide(grown), spread_ref[step])
        grown = jnp.concatenate([grown] + [more[:, j * LANES : (j + 1) * LANES] for j in range(3)], 0)
    out_ref[...] = swept_ref[...] + grown


def on_device(observations, sensor_map, noise_precision, availability, decay_rate, prior_mean):
    modes = sensor_map.shape[1]
    rows = observations.shape[0]
    z, y, c, x = (lax.axis_index(a) for a in "zycx")
    k = (z * NY + y) * NC + c
    place = jnp.stack([x, k, z, c, y]).astype(jnp.int32)
    square = f32(modes, modes)
    packet = pack(availability, noise_precision, sensor_map)
    packets = [packet] + [xor_over_x(packet, d) for d in (1, 2, 3)]
    kept, half = gather(place, packets)
    sent = once(by_taker(observations), *packets[1:])
    received = lax.all_to_all(sent, ("y", "c", "x"), split_axis=0, concat_axis=0, tiled=True)

    for flip in (1, 2, 4):
        kept = kept + lax.ppermute(kept, "z", [(i, i ^ flip) for i in range(NZ)])
    plane, masks = local(
        mask_kernel, "masks", [place], [kept, half, lax.ppermute(half, "c", [(0, 1), (1, 0)])],
        [jax.ShapeDtypeStruct((2 * modes, NX * NY * modes // 2), jnp.bfloat16), f32(NZ, NX * NY * modes // 2)], 1 << 20,
    )

    info = weigh(availability, noise_precision, sensor_map)
    infos = [info] + [xor_over_x(info, d) for d in (1, 2, 3)]

    partial, done = info_rows(place, masks, plane, received.reshape(NY * NC, NX, NZ, rows // 2, LANES))
    partial = lax.all_to_all(partial, "z", split_axis=0, concat_axis=0, tiled=True)
    piece = jnp.sum(partial, 0)
    pieces = [piece] + [xor_over_x(piece, d) for d in (1, 2, 3)]

    retain = jnp.exp(-decay_rate)
    powers, total = local(
        power_kernel, "powers", [],
        infos + [decay_rate[None, :], jnp.broadcast_to(retain[:, None], (modes, modes))],
        [f32(LEVELS, modes, modes), square], 4 * 10**10, tokens=[done],
    )
    steps = LEVELS // 2
    adding, spreading = local(
        factor_kernel, "factors", [], [powers],
        [
            jax.ShapeDtypeStruct((steps, 9 * modes, modes), jnp.bfloat16),
            jax.ShapeDtypeStruct((steps, 3 * modes, 3 * modes), jnp.bfloat16),
        ],
        4 * 6 * 2 * modes**3,
    )
    terms = jax.ShapeDtypeStruct((3 * modes, modes), jnp.bfloat16)
    got = lax.ppermute(total, "c", [(0, 1), (1, 0)])
    total, lead, rest, *pair_terms = local(
        pair_kernel, "pairs", [place], [total, got], [square] * 3 + [terms] * 2, 6 * 2 * modes**3
    )
    leads, rests = [pair_terms[0]], [pair_terms[1]]
    got = [lax.ppermute(total, "y", [(i, i ^ d) for i in range(NY)]) for d in (1, 2, 3)]
    total, lead, rest, *quad_terms = local(
        quad_kernel, "quads", [y.astype(jnp.int32)[None]], [total] + got + [lead, rest],
        [square] * 3 + [terms] * 4, 5 * 6 * 2 * modes**3,
    )
    leads += quad_terms[::2]
    rests += quad_terms[1::2]
    got = [lax.ppermute(total, "z", [(i, i ^ d) for i in range(NZ)]) for d in (1, 2, 3)]

    drive, tail, near = local(
        tail_kernel, "tail", [place],
        pieces + [decay_rate[None, :], prior_mean[None, :], adding, spreading] + rests,
        [f32(STEPS, modes), f32(8, modes), f32(NK, modes)], 8 * 6 * 2 * modes**3,
    )
    *far_terms, sends = local(
        far_kernel, "far", [place], [total] + got + [lead, rest, tail, near],
        [terms] * 2 + [f32(NK, modes)], 5 * 6 * 2 * modes**3,
    )
    leads += far_terms

    offsets = lax.all_to_all(sends, ("z", "y", "c"), split_axis=0, concat_axis=0, tiled=True)
    (swept,) = local(
        sweep_kernel, "sweep", [], [drive, spreading], [f32(STEPS, modes)], 8 * 12 * 2 * modes**3
    )
    (states,) = local(
        state_kernel, "states", [place], [offsets, spreading, swept] + leads,
        [f32(STEPS, modes)], 15 * 6 * 2 * modes**3,
    )
    return states


def solution(mesh):
    fine = Mesh(mesh.devices.reshape(NZ, NY, NC, NX), ("z", "y", "c", "x"))
    return jax.shard_map(
        on_device,
        mesh=fine,
        in_specs=(
            P(("x", "z", "y", "c"), None),
            P("x", None),
            P("x", None, None),
            P(("z", "y", "c"), "x"),
            P(),
            P(),
        ),
        out_specs=P(("z", "y", "c"), None),
        check_vma=False,
    )
```

```python
import jax
import jax.numpy as jnp
from jax import lax
from jax.experimental import pallas as pl
from jax.experimental.pallas import tpu as pltpu
from jax.sharding import Mesh, PartitionSpec as P

NZ, NY, NC, NX = 8, 4, 2, 4
NK = NZ * NY * NC
STEPS = 256
LEVELS = 8
SCAN = 6
LANES = 128
HIGHEST = lax.Precision.HIGHEST
WHOLE = pl.BlockSpec(memory_space=pltpu.VMEM)
SCALARS = pl.BlockSpec(memory_space=pltpu.SMEM)


def dot(a, b):
    return jnp.dot(a, b, precision=HIGHEST, preferred_element_type=jnp.float32)


def f32(*shape):
    return jax.ShapeDtypeStruct(shape, jnp.float32)


def local(body, name, scalars, arrays, outs, flops, tokens=(), scratch=(), moved=1 << 20):
    inputs = len(scalars) + len(arrays)

    def call(*refs):
        body(*refs[:inputs], *refs[inputs + len(tokens) :])

    return pl.pallas_call(
        call,
        name=name,
        out_shape=outs,
        in_specs=[SCALARS] * len(scalars)
        + [WHOLE] * (len(arrays) + len(tokens)),
        out_specs=[WHOLE] * len(outs),
        scratch_shapes=list(scratch),
        cost_estimate=pl.CostEstimate(flops=flops, bytes_accessed=moved, transcendentals=0),
        compiler_params=pltpu.CompilerParams(vmem_limit_bytes=32 << 20),
    )(*scalars, *arrays, *tokens)


def split(a):
    high = a.astype(jnp.bfloat16)
    return high, (a - high.astype(jnp.float32)).astype(jnp.bfloat16)


def wide(a):
    high, low = split(a)
    return jnp.concatenate([high, low, high], 1)


def tall(a):
    high, low = split(a)
    return jnp.concatenate([high, high, low], 0)


def times(terms, factor):
    return jnp.dot(terms, factor, preferred_element_type=jnp.float32)


def xor_over_x(block, distance):
    return lax.ppermute(block, "x", [(i, i ^ distance) for i in range(NX)])


def order_kernel(rows_ref, out_ref):
    half, side = rows_ref.shape[0] // 2, LANES // 2
    for k in range(NZ):
        for j in range(NY * NC):
            for pair in range(2):
                lane = ((k * NY * NC + j) * 2 + pair) * LANES
                upper = rows_ref[:half, lane : lane + LANES]
                lower = rows_ref[half:, lane : lane + LANES]
                out_ref[j, 2 * pair, k] = jnp.concatenate([upper[:, :side], lower[:, :side]], 1)
                out_ref[j, 2 * pair + 1, k] = jnp.concatenate([upper[:, side:], lower[:, side:]], 1)


def by_taker(observations):
    half = observations.shape[0] // 2
    out = pl.pallas_call(
        order_kernel,
        name="by_taker",
        out_shape=jax.ShapeDtypeStruct((NY * NC, NX, NZ, half, LANES), jnp.bfloat16),
        in_specs=[WHOLE],
        out_specs=WHOLE,
        cost_estimate=pl.CostEstimate(flops=0, bytes_accessed=4 << 20, transcendentals=0),
        compiler_params=pltpu.CompilerParams(vmem_limit_bytes=32 << 20),
    )(observations)
    return out.reshape(NY * NC * NX, NZ * half, LANES)


def pack_kernel(kept_ref, noise_ref, map_ref, out_ref, noise_held, map_held, sems):
    first = lax.axis_index("z") * NY + lax.axis_index("c") * 2
    copies = [
        pltpu.make_async_copy(noise_ref.at[pl.ds(first, 2)], noise_held, sems.at[0]),
        pltpu.make_async_copy(map_ref.at[pl.ds(first * LANES, 2 * LANES)], map_held, sems.at[1]),
    ]
    for copy in copies:
        copy.start()
    blocks = kept_ref.shape[1]
    lane = lax.broadcasted_iota(jnp.int32, (16, LANES), 1) - lax.axis_index("x") * blocks
    row = jnp.zeros((16, LANES), jnp.float32)
    for b in range(blocks):
        row = jnp.where(lane == b, kept_ref[0, b].astype(jnp.float32), row)
    out_ref[LANES:, :LANES] = row.astype(jnp.bfloat16)
    out_ref[LANES:, LANES:] = jnp.zeros((16, LANES), jnp.bfloat16)
    for copy in copies:
        copy.wait()
    for b in range(2):
        weights = jnp.dot(
            noise_held[b], map_held[b * LANES : (b + 1) * LANES, :], preferred_element_type=jnp.float32
        )
        out_ref[:LANES, b * LANES : (b + 1) * LANES] = weights.T.astype(jnp.bfloat16)


def pack(availability, noise_precision, sensor_map):
    return pl.pallas_call(
        pack_kernel,
        name="pack",
        out_shape=jax.ShapeDtypeStruct((LANES + 16, 2 * LANES), jnp.bfloat16),
        in_specs=[SCALARS, pl.BlockSpec(memory_space=pl.ANY), pl.BlockSpec(memory_space=pl.ANY)],
        out_specs=WHOLE,
        scratch_shapes=[
            pltpu.VMEM((2, LANES, LANES), jnp.bfloat16),
            pltpu.VMEM((2 * LANES, LANES), jnp.bfloat16),
            pltpu.SemaphoreType.DMA((2,)),
        ],
        cost_estimate=pl.CostEstimate(flops=1 << 23, bytes_accessed=1 << 18, transcendentals=0),
    )(availability, noise_precision, sensor_map)


def gather_kernel(place_ref, own_ref, one_ref, two_ref, three_ref, kept_ref, half_ref, held_ref, sems):
    copies = [
        pltpu.make_async_copy(ref, held_ref.at[r], sems.at[r])
        for r, ref in enumerate((own_ref, one_ref, two_ref, three_ref))
    ]
    for copy in copies:
        copy.start()
    for copy in copies:
        copy.wait()
    kept = sum(held_ref[r, LANES:, :LANES].astype(jnp.float32)[:NZ] for r in range(NX))
    at = lax.broadcasted_iota(jnp.int32, (NZ, LANES), 0)
    kept_ref[...] = jnp.where(at == place_ref[2], kept, 0.0)
    for r in range(NX):
        half_ref[:, 2 * r * LANES : 2 * (r + 1) * LANES] = held_ref[r, :LANES]


def gather(place, packets):
    return pl.pallas_call(
        gather_kernel,
        name="gather",
        out_shape=[f32(NZ, LANES), jax.ShapeDtypeStruct((LANES, NX * 2 * LANES), jnp.bfloat16)],
        in_specs=[SCALARS] + [pl.BlockSpec(memory_space=pl.ANY)] * NX,
        out_specs=[WHOLE] * 2,
        scratch_shapes=[
            pltpu.VMEM((NX,) + packets[0].shape, jnp.bfloat16),
            pltpu.SemaphoreType.DMA((NX,)),
        ],
        cost_estimate=pl.CostEstimate(flops=0, bytes_accessed=1 << 20, transcendentals=0),
    )(place, *packets)


def weigh_kernel(kept_ref, noise_ref, map_ref, out_ref):
    step = pl.program_id(0)
    blocks, sblk = noise_ref.shape[0], noise_ref.shape[1]
    parts = []
    for b in range(blocks):
        weights = jnp.dot(
            noise_ref[b], map_ref[b * sblk : (b + 1) * sblk, :], preferred_element_type=jnp.float32
        )
        parts.append((weights * kept_ref[0, step * blocks + b].astype(jnp.float32)).astype(jnp.bfloat16))
    share = lax.dot_general(
        jnp.concatenate(parts, 0), map_ref[...], (((0,), (0,)), ((), ())), preferred_element_type=jnp.float32
    )

    @pl.when(step == 0)
    def _():
        out_ref[...] = share

    @pl.when(step > 0)
    def _():
        out_ref[...] += share


def weigh(availability, noise_precision, sensor_map):
    blocks, sblk, _ = noise_precision.shape
    step = blocks // 4
    return pl.pallas_call(
        weigh_kernel,
        name="weigh",
        grid=(4,),
        out_shape=f32(LANES, LANES),
        in_specs=[
            SCALARS,
            pl.BlockSpec((step, sblk, sblk), lambda i: (i, 0, 0)),
            pl.BlockSpec((step * sblk, LANES), lambda i: (i, 0)),
        ],
        out_specs=pl.BlockSpec((LANES, LANES), lambda i: (0, 0)),
        cost_estimate=pl.CostEstimate(flops=4 * blocks * sblk**3, bytes_accessed=2 << 20, transcendentals=0),
    )(availability, noise_precision, sensor_map)


def power_kernel(own_ref, one_ref, two_ref, three_ref, decay_ref, retain_ref, out_ref, block_ref):
    info = (own_ref[...] + one_ref[...]) + (two_ref[...] + three_ref[...])
    row = lax.broadcasted_iota(jnp.int32, info.shape, 0)
    column = lax.broadcasted_iota(jnp.int32, info.shape, 1)
    identity = jnp.where(row == column, 1.0, 0.0)
    power = (identity - decay_ref[...] * info) * retain_ref[...]
    for level in range(LEVELS):
        out_ref[level] = power
        power = dot(power, power)
    block_ref[...] = power


def factor_kernel(power_ref, add_ref, spread_ref, token_ref):
    token_ref[...] = jnp.zeros((8, LANES), jnp.float32)
    for step in range(LEVELS // 2):
        one, two = power_ref[2 * step], power_ref[2 * step + 1]
        for j, power in enumerate((one, two, dot(one, two))):
            terms = tall(power)
            add_ref[step, (2 - j) * 3 * LANES : (3 - j) * 3 * LANES] = terms
            spread_ref[step, :, j * LANES : (j + 1) * LANES] = terms


def once_kernel(array_ref, *refs):
    pass


def once(array, *tokens):
    return pl.pallas_call(
        once_kernel,
        name="once",
        out_shape=jax.ShapeDtypeStruct(array.shape, array.dtype),
        in_specs=[pl.BlockSpec(memory_space=pl.ANY)] * (1 + len(tokens)),
        out_specs=pl.BlockSpec(memory_space=pl.ANY),
        input_output_aliases={0: 0},
        compiler_params=pltpu.CompilerParams(vmem_limit_bytes=60 << 20),
    )(array, *tokens)


def factor_kernel(power_ref, add_ref, spread_ref, token_ref):
    token_ref[...] = jnp.zeros((8, LANES), jnp.float32)
    for step in range(LEVELS // 2):
        one, two = power_ref[2 * step], power_ref[2 * step + 1]
        for j, power in enumerate((one, two, dot(one, two))):
            terms = tall(power)
            add_ref[step, (2 - j) * 3 * LANES : (3 - j) * 3 * LANES] = terms
            spread_ref[step, :, j * LANES : (j + 1) * LANES] = terms


def joined(upper, total, beside, lead, rest):
    both = dot(jnp.where(upper, beside, total), jnp.where(upper, total, beside))
    new = dot(jnp.where(upper, beside, rest), jnp.where(upper, lead, beside))
    return both, jnp.where(upper, new, lead), jnp.where(upper, rest, new)


def pair_kernel(place_ref, total_ref, got_ref, total_out, lead_out, rest_out, lead_terms, rest_terms):
    row = lax.broadcasted_iota(jnp.int32, (LANES, LANES), 0)
    column = lax.broadcasted_iota(jnp.int32, (LANES, LANES), 1)
    identity = jnp.where(row == column, 1.0, 0.0)
    upper = place_ref[1] % 2 == 1
    total, got = total_ref[...], got_ref[...]
    lead, rest = jnp.where(upper, got, identity), jnp.where(upper, identity, got)
    total_out[...] = dot(jnp.where(upper, got, total), jnp.where(upper, total, got))
    lead_out[...], rest_out[...] = lead, rest
    lead_terms[...], rest_terms[...] = tall(lead), tall(rest)


def quad_kernel(bits_ref, total_ref, one_ref, two_ref, three_ref, lead_ref, rest_ref, total_out, lead_out, rest_out, *terms):
    odd, upper = bits_ref[0] % 2 == 1, bits_ref[0] % 4 >= 2
    two, three = two_ref[...], three_ref[...]
    total, lead, rest = joined(odd, total_ref[...], one_ref[...], lead_ref[...], rest_ref[...])
    terms[0][...], terms[1][...] = tall(lead), tall(rest)
    beside = dot(jnp.where(odd, three, two), jnp.where(odd, two, three))
    total, lead, rest = joined(upper, total, beside, lead, rest)
    terms[2][...], terms[3][...] = tall(lead), tall(rest)
    total_out[...], lead_out[...], rest_out[...] = total, lead, rest


def mask_kernel(place_ref, kept_ref, own_ref, other_ref, plane_ref, mask_ref):
    x, z, c = place_ref[0], place_ref[2], place_ref[3]
    width = NY * LANES
    kept = kept_ref[...].astype(jnp.bfloat16)
    block = lax.broadcasted_iota(jnp.int32, (LANES, width // 2), 0)
    lane = lax.broadcasted_iota(jnp.int32, (LANES, width // 2), 1) // (LANES // 2)
    source = lax.broadcasted_iota(jnp.int32, (width, width // 2), 0)
    target = lax.broadcasted_iota(jnp.int32, (width, width // 2), 1)
    picks = [
        jnp.where(source == target // 32 * 64 + target % 32 + 32 * side, 1.0, 0.0).astype(jnp.bfloat16)
        for side in range(2)
    ]
    for r in range(NX):
        lanes = slice(r * width // 2, (r + 1) * width // 2)
        own, other = own_ref[:, lanes], other_ref[:, lanes]
        whole = jnp.concatenate([jnp.where(c == 0, own, other), jnp.where(c == 0, other, own)], 1)
        for side in range(2):
            plane_ref[side * LANES : (side + 1) * LANES, lanes] = jnp.dot(
                whole, picks[side], preferred_element_type=jnp.float32
            ).astype(jnp.bfloat16)
        spread = jnp.where(block == (x ^ r) * (NZ * NY) + z * NY + lane, 1.0, 0.0).astype(jnp.bfloat16)
        mask_ref[:, lanes] = jnp.dot(kept, spread, preferred_element_type=jnp.float32)


def rows_kernel(place_ref, mask_ref, plane_ref, got_ref, out_ref, token_ref):
    x = place_ref[0]
    token_ref[...] = jnp.zeros((8, LANES), jnp.float32)
    rows = plane_ref.shape[1] // NX
    side = LANES // 2
    left = lax.broadcasted_iota(jnp.int32, (LANES, LANES), 1) < side
    for k in range(NZ):
        weights = plane_ref[...] * mask_ref[k : k + 1, :].astype(jnp.bfloat16)
        readings = jnp.concatenate([got_ref[:, x ^ r, k].reshape(rows, LANES) for r in range(NX)], 0)
        both = jnp.dot(weights, readings, preferred_element_type=jnp.float32)
        upper, lower = both[:LANES], both[LANES:]
        if k % 2 == 0:
            first = upper + pltpu.roll(lower, side, 1)
        else:
            second = lower + pltpu.roll(upper, side, 1)
            pair = jnp.where(left, first, second).T
            out_ref[k - 1], out_ref[k] = pair[:side], pair[side:]


def info_rows(place, masks, plane, received):
    return pl.pallas_call(
        rows_kernel,
        name="rows",
        out_shape=[f32(NZ, LANES // 2, LANES), f32(8, LANES)],
        in_specs=[SCALARS, WHOLE, WHOLE, WHOLE],
        out_specs=[WHOLE] * 2,
        cost_estimate=pl.CostEstimate(flops=1 << 28, bytes_accessed=3 << 20, transcendentals=0),
        compiler_params=pltpu.CompilerParams(vmem_limit_bytes=32 << 20),
    )(place, masks, plane, received)


def tail_kernel(place_ref, a_ref, b_ref, c_ref, d_ref, decay_ref, prior_ref, add_ref, spread_ref, *refs):
    rest_refs, (drive_ref, tail_ref, near_ref) = refs[:3], refs[3:]
    x = place_ref[0]
    rows = a_ref.shape[0]
    for r, ref in enumerate((a_ref, b_ref, c_ref, d_ref)):
        drive_ref[pl.ds(pl.multiple_of((x ^ r) * rows, rows), rows), :] = ref[...] * decay_ref[...]
    pushed = times(wide(prior_ref[...]), spread_ref[0, :, :LANES])
    drive_ref[:1] += jnp.where(place_ref[1] == 0, pushed, 0.0)
    tail = drive_ref[...]
    for step in reversed(range(LEVELS // 2)):
        n = 4**step
        terms = jnp.concatenate([wide(tail[j * n : (j + 1) * n]) for j in range(3)], 1)
        tail = times(terms, add_ref[step]) + tail[3 * n :]
    tail_ref[...] = jnp.broadcast_to(tail, (8, LANES))
    near_ref[...] = onward(place_ref[1], tail, jnp.broadcast_to(tail, (NK, LANES)), 1, [ref[...] for ref in rest_refs])


def onward(k, tail, sends, level, factors):
    to = lax.broadcasted_iota(jnp.int32, (NK, LANES), 0) ^ k
    terms = wide(tail)
    for step, factor in enumerate(factors):
        sends = jnp.where(to >= 2 ** (level + step), times(terms, factor), sends)
    return sends


def far_kernel(place_ref, one_ref, two_ref, three_ref, lead_ref, rest_ref, tail_ref, near_ref, four_ref, five_ref, send_ref):
    odd, upper = place_ref[2] % 2 == 1, place_ref[2] % 4 >= 2
    one, two, three = one_ref[...], two_ref[...], three_ref[...]
    lead, rest = lead_ref[...], rest_ref[...]
    beside = times(wide(jnp.where(odd, three, two)), tall(jnp.where(odd, two, three)))
    new = times(wide(jnp.where(odd, one, rest)), tall(jnp.where(odd, lead, one)))
    lead, rest = jnp.where(odd, new, lead), jnp.where(odd, rest, new)
    four_ref[...] = tall(lead)
    factors = [tall(rest)]
    new = times(wide(jnp.where(upper, beside, rest)), tall(jnp.where(upper, lead, beside)))
    five_ref[...] = tall(jnp.where(upper, new, lead))
    factors.append(tall(jnp.where(upper, rest, new)))
    send_ref[...] = onward(place_ref[1], tail_ref[:1], near_ref[...], 4, factors)


def sweep_kernel(drive_ref, spread_ref, out_ref):
    swept = drive_ref[...]
    row = lax.broadcasted_iota(jnp.int32, (STEPS, LANES), 0)
    for step in range(LEVELS // 2):
        for side in range(2):
            shift = 4**step * (1 + side)
            before = jnp.where(row >= shift, pltpu.roll(swept, shift, 0), 0.0)
            swept += times(wide(before), spread_ref[step, :, side * LANES : (side + 1) * LANES])
    out_ref[...] = swept


def step_kernel(power_ref, *refs):
    step = power_ref[...]
    for lead_ref, out_ref in zip(refs[: SCAN - 1], refs[SCAN - 1 :]):
        lead = lead_ref[:LANES].astype(jnp.float32) + lead_ref[2 * LANES :].astype(jnp.float32)
        out_ref[...] = tall(dot(lead, step))


def state_kernel(place_ref, offsets_ref, spread_ref, swept_ref, *refs):
    lead_refs, out_ref = refs[:-1], refs[-1]
    k = place_ref[1]
    index = lax.broadcasted_iota(jnp.int32, (NK, LANES), 0)
    apart = jnp.where(index < k, index ^ k, 0)
    offsets = offsets_ref[...]
    parts = []
    for level in range(SCAN):
        chosen = (apart >= 2**level) & (apart < 2 ** (level + 1))
        parts.append(jnp.sum(jnp.where(chosen, offsets, 0.0), 0, keepdims=True))
    grown = times(wide(parts[0]), spread_ref[0, :, :LANES])
    for level in range(1, SCAN):
        grown += times(wide(parts[level]), lead_refs[level - 1][...])
    for step in range(LEVELS // 2):
        more = times(wide(grown), spread_ref[step])
        grown = jnp.concatenate([grown] + [more[:, j * LANES : (j + 1) * LANES] for j in range(3)], 0)
    out_ref[...] = swept_ref[...] + grown


def on_device(observations, sensor_map, noise_precision, availability, decay_rate, prior_mean):
    modes = sensor_map.shape[1]
    rows = observations.shape[0]
    z, y, c, x = (lax.axis_index(a) for a in "zycx")
    k = (z * NY + y) * NC + c
    place = jnp.stack([x, k, z, c, y]).astype(jnp.int32)
    square = f32(modes, modes)
    packet = pack(availability, noise_precision, sensor_map)
    packets = [packet] + [xor_over_x(packet, d) for d in (1, 2, 3)]
    kept, half = gather(place, packets)
    sent = once(by_taker(observations), *packets[1:])
    received = lax.all_to_all(sent, ("y", "c", "x"), split_axis=0, concat_axis=0, tiled=True)

    for flip in (1, 2, 4):
        kept = kept + lax.ppermute(kept, "z", [(i, i ^ flip) for i in range(NZ)])
    plane, masks = local(
        mask_kernel, "masks", [place], [kept, half, lax.ppermute(half, "c", [(0, 1), (1, 0)])],
        [jax.ShapeDtypeStruct((2 * modes, NX * NY * modes // 2), jnp.bfloat16), f32(NZ, NX * NY * modes // 2)], 1 << 20,
    )

    info = weigh(availability, noise_precision, sensor_map)
    infos = [info] + [xor_over_x(info, d) for d in (1, 2, 3)]

    partial, done = info_rows(place, masks, plane, received.reshape(NY * NC, NX, NZ, rows // 2, LANES))
    partial = lax.all_to_all(partial, "z", split_axis=0, concat_axis=0, tiled=True)
    piece = jnp.sum(partial, 0)
    pieces = [piece] + [xor_over_x(piece, d) for d in (1, 2, 3)]

    retain = jnp.exp(-decay_rate)
    powers, total = local(
        power_kernel, "powers", [],
        infos + [decay_rate[None, :], jnp.broadcast_to(retain[:, None], (modes, modes))],
        [f32(LEVELS, modes, modes), square], 4 * 10**10, tokens=[done],
    )
    steps = LEVELS // 2
    adding, spreading, ready = local(
        factor_kernel, "factors", [], [powers],
        [
            jax.ShapeDtypeStruct((steps, 9 * modes, modes), jnp.bfloat16),
            jax.ShapeDtypeStruct((steps, 3 * modes, 3 * modes), jnp.bfloat16),
            f32(8, modes),
        ],
        4 * 6 * 2 * modes**3,
    )
    terms = jax.ShapeDtypeStruct((3 * modes, modes), jnp.bfloat16)
    got = lax.ppermute(total, "c", [(0, 1), (1, 0)])
    total, lead, rest, *pair_terms = local(
        pair_kernel, "pairs", [place], [total, got], [square] * 3 + [terms] * 2, 6 * 2 * modes**3
    )
    leads, rests = [pair_terms[0]], [pair_terms[1]]
    got = [lax.ppermute(total, "y", [(i, i ^ d) for i in range(NY)]) for d in (1, 2, 3)]
    total, lead, rest, *quad_terms = local(
        quad_kernel, "quads", [y.astype(jnp.int32)[None]], [total] + got + [lead, rest],
        [square] * 3 + [terms] * 4, 5 * 6 * 2 * modes**3, tokens=[ready],
    )
    leads += quad_terms[::2]
    rests += quad_terms[1::2]
    got = [lax.ppermute(total, "z", [(i, i ^ d) for i in range(NZ)]) for d in (1, 2, 3)]

    drive, tail, near = local(
        tail_kernel, "tail", [place],
        pieces + [decay_rate[None, :], prior_mean[None, :], adding, spreading] + rests,
        [f32(STEPS, modes), f32(8, modes), f32(NK, modes)], 8 * 6 * 2 * modes**3,
    )
    *far_terms, sends = local(
        far_kernel, "far", [place], got + [lead, rest, tail, near],
        [terms] * 2 + [f32(NK, modes)], 5 * 6 * 2 * modes**3,
    )
    leads += far_terms

    offsets = lax.all_to_all(sends, ("z", "y", "c"), split_axis=0, concat_axis=0, tiled=True)
    (swept,) = local(
        sweep_kernel, "sweep", [], [drive, spreading], [f32(STEPS, modes)], 8 * 12 * 2 * modes**3
    )
    leads = list(local(
        step_kernel, "steps", [], [powers[0]] + leads, [terms] * (SCAN - 1), 5 * 6 * 2 * modes**3, tokens=[swept]
    ))
    (states,) = local(
        state_kernel, "states", [place], [offsets, spreading, swept] + leads,
        [f32(STEPS, modes)], 15 * 6 * 2 * modes**3,
    )
    return states


def solution(mesh):
    fine = Mesh(mesh.devices.reshape(NZ, NY, NC, NX), ("z", "y", "c", "x"))
    return jax.shard_map(
        on_device,
        mesh=fine,
        in_specs=(
            P(("x", "z", "y", "c"), None),
            P("x", None),
            P("x", None, None),
            P(("z", "y", "c"), "x"),
            P(),
            P(),
        ),
        out_specs=P(("z", "y", "c"), None),
        check_vma=False,
    )
```

```python
import jax
import jax.numpy as jnp
from jax import lax
from jax.experimental import pallas as pl
from jax.experimental.pallas import tpu as pltpu
from jax.sharding import Mesh, PartitionSpec as P

NZ, NY, NC, NX = 8, 4, 2, 4
NK = NZ * NY * NC
STEPS = 256
LEVELS = 8
SCAN = 6
LANES = 128
HIGHEST = lax.Precision.HIGHEST
WHOLE = pl.BlockSpec(memory_space=pltpu.VMEM)
SCALARS = pl.BlockSpec(memory_space=pltpu.SMEM)


def dot(a, b):
    return jnp.dot(a, b, precision=HIGHEST, preferred_element_type=jnp.float32)


def f32(*shape):
    return jax.ShapeDtypeStruct(shape, jnp.float32)


def local(body, name, scalars, arrays, outs, flops, tokens=(), scratch=(), moved=1 << 20):
    inputs = len(scalars) + len(arrays)

    def call(*refs):
        body(*refs[:inputs], *refs[inputs + len(tokens) :])

    return pl.pallas_call(
        call,
        name=name,
        out_shape=outs,
        in_specs=[SCALARS] * len(scalars)
        + [WHOLE] * (len(arrays) + len(tokens)),
        out_specs=[WHOLE] * len(outs),
        scratch_shapes=list(scratch),
        cost_estimate=pl.CostEstimate(flops=flops, bytes_accessed=moved, transcendentals=0),
        compiler_params=pltpu.CompilerParams(vmem_limit_bytes=32 << 20),
    )(*scalars, *arrays, *tokens)


def split(a):
    high = a.astype(jnp.bfloat16)
    return high, (a - high.astype(jnp.float32)).astype(jnp.bfloat16)


def wide(a):
    high, low = split(a)
    return jnp.concatenate([high, low, high], 1)


def tall(a):
    high, low = split(a)
    return jnp.concatenate([high, high, low], 0)


def times(terms, factor):
    return jnp.dot(terms, factor, preferred_element_type=jnp.float32)


def xor_over_x(block, distance):
    return lax.ppermute(block, "x", [(i, i ^ distance) for i in range(NX)])


def order_kernel(rows_ref, out_ref):
    half, side = rows_ref.shape[0] // 2, LANES // 2
    for k in range(NZ):
        for j in range(NY * NC):
            for pair in range(2):
                lane = ((k * NY * NC + j) * 2 + pair) * LANES
                upper = rows_ref[:half, lane : lane + LANES]
                lower = rows_ref[half:, lane : lane + LANES]
                out_ref[j, 2 * pair, k] = jnp.concatenate([upper[:, :side], lower[:, :side]], 1)
                out_ref[j, 2 * pair + 1, k] = jnp.concatenate([upper[:, side:], lower[:, side:]], 1)


def by_taker(observations):
    half = observations.shape[0] // 2
    out = pl.pallas_call(
        order_kernel,
        name="by_taker",
        out_shape=jax.ShapeDtypeStruct((NY * NC, NX, NZ, half, LANES), jnp.bfloat16),
        in_specs=[WHOLE],
        out_specs=WHOLE,
        cost_estimate=pl.CostEstimate(flops=0, bytes_accessed=4 << 20, transcendentals=0),
        compiler_params=pltpu.CompilerParams(vmem_limit_bytes=32 << 20),
    )(observations)
    return out.reshape(NY * NC * NX, NZ * half, LANES)


def pack_kernel(kept_ref, noise_ref, map_ref, out_ref, noise_held, map_held, sems):
    first = lax.axis_index("z") * NY + lax.axis_index("c") * 2
    copies = [
        pltpu.make_async_copy(noise_ref.at[pl.ds(first, 2)], noise_held, sems.at[0]),
        pltpu.make_async_copy(map_ref.at[pl.ds(first * LANES, 2 * LANES)], map_held, sems.at[1]),
    ]
    for copy in copies:
        copy.start()
    blocks = kept_ref.shape[1]
    lane = lax.broadcasted_iota(jnp.int32, (16, LANES), 1) - lax.axis_index("x") * blocks
    row = jnp.zeros((16, LANES), jnp.float32)
    for b in range(blocks):
        row = jnp.where(lane == b, kept_ref[0, b].astype(jnp.float32), row)
    out_ref[LANES:, :LANES] = row.astype(jnp.bfloat16)
    out_ref[LANES:, LANES:] = jnp.zeros((16, LANES), jnp.bfloat16)
    for copy in copies:
        copy.wait()
    for b in range(2):
        weights = jnp.dot(
            noise_held[b], map_held[b * LANES : (b + 1) * LANES, :], preferred_element_type=jnp.float32
        )
        out_ref[:LANES, b * LANES : (b + 1) * LANES] = weights.T.astype(jnp.bfloat16)


def pack(availability, noise_precision, sensor_map):
    return pl.pallas_call(
        pack_kernel,
        name="pack",
        out_shape=jax.ShapeDtypeStruct((LANES + 16, 2 * LANES), jnp.bfloat16),
        in_specs=[SCALARS, pl.BlockSpec(memory_space=pl.ANY), pl.BlockSpec(memory_space=pl.ANY)],
        out_specs=WHOLE,
        scratch_shapes=[
            pltpu.VMEM((2, LANES, LANES), jnp.bfloat16),
            pltpu.VMEM((2 * LANES, LANES), jnp.bfloat16),
            pltpu.SemaphoreType.DMA((2,)),
        ],
        cost_estimate=pl.CostEstimate(flops=1 << 23, bytes_accessed=1 << 18, transcendentals=0),
    )(availability, noise_precision, sensor_map)


def gather_kernel(place_ref, own_ref, one_ref, two_ref, three_ref, kept_ref, half_ref, held_ref, sems):
    copies = [
        pltpu.make_async_copy(ref, held_ref.at[r], sems.at[r])
        for r, ref in enumerate((own_ref, one_ref, two_ref, three_ref))
    ]
    for copy in copies:
        copy.start()
    for copy in copies:
        copy.wait()
    kept = sum(held_ref[r, LANES:, :LANES].astype(jnp.float32)[:NZ] for r in range(NX))
    at = lax.broadcasted_iota(jnp.int32, (NZ, LANES), 0)
    kept_ref[...] = jnp.where(at == place_ref[2], kept, 0.0)
    for r in range(NX):
        half_ref[:, 2 * r * LANES : 2 * (r + 1) * LANES] = held_ref[r, :LANES]


def gather(place, packets):
    return pl.pallas_call(
        gather_kernel,
        name="gather",
        out_shape=[f32(NZ, LANES), jax.ShapeDtypeStruct((LANES, NX * 2 * LANES), jnp.bfloat16)],
        in_specs=[SCALARS] + [pl.BlockSpec(memory_space=pl.ANY)] * NX,
        out_specs=[WHOLE] * 2,
        scratch_shapes=[
            pltpu.VMEM((NX,) + packets[0].shape, jnp.bfloat16),
            pltpu.SemaphoreType.DMA((NX,)),
        ],
        cost_estimate=pl.CostEstimate(flops=0, bytes_accessed=1 << 20, transcendentals=0),
    )(place, *packets)


def weigh_kernel(kept_ref, noise_ref, map_ref, out_ref):
    step = pl.program_id(0)
    blocks, sblk = noise_ref.shape[0], noise_ref.shape[1]
    parts = []
    for b in range(blocks):
        weights = jnp.dot(
            noise_ref[b], map_ref[b * sblk : (b + 1) * sblk, :], preferred_element_type=jnp.float32
        )
        parts.append((weights * kept_ref[0, step * blocks + b].astype(jnp.float32)).astype(jnp.bfloat16))
    share = lax.dot_general(
        jnp.concatenate(parts, 0), map_ref[...], (((0,), (0,)), ((), ())), preferred_element_type=jnp.float32
    )

    @pl.when(step == 0)
    def _():
        out_ref[...] = share

    @pl.when(step > 0)
    def _():
        out_ref[...] += share


def weigh(availability, noise_precision, sensor_map):
    blocks, sblk, _ = noise_precision.shape
    step = blocks // 4
    return pl.pallas_call(
        weigh_kernel,
        name="weigh",
        grid=(4,),
        out_shape=f32(LANES, LANES),
        in_specs=[
            SCALARS,
            pl.BlockSpec((step, sblk, sblk), lambda i: (i, 0, 0)),
            pl.BlockSpec((step * sblk, LANES), lambda i: (i, 0)),
        ],
        out_specs=pl.BlockSpec((LANES, LANES), lambda i: (0, 0)),
        cost_estimate=pl.CostEstimate(flops=4 * blocks * sblk**3, bytes_accessed=2 << 20, transcendentals=0),
    )(availability, noise_precision, sensor_map)


def power_kernel(own_ref, one_ref, two_ref, three_ref, decay_ref, retain_ref, out_ref, block_ref):
    info = (own_ref[...] + one_ref[...]) + (two_ref[...] + three_ref[...])
    row = lax.broadcasted_iota(jnp.int32, info.shape, 0)
    column = lax.broadcasted_iota(jnp.int32, info.shape, 1)
    identity = jnp.where(row == column, 1.0, 0.0)
    power = (identity - decay_ref[...] * info) * retain_ref[...]
    for level in range(LEVELS):
        out_ref[level] = power
        power = dot(power, power)
    block_ref[...] = power


def factor_kernel(power_ref, add_ref, spread_ref, token_ref):
    token_ref[...] = jnp.zeros((8, LANES), jnp.float32)
    for step in range(LEVELS // 2):
        one, two = power_ref[2 * step], power_ref[2 * step + 1]
        for j, power in enumerate((one, two, dot(one, two))):
            terms = tall(power)
            add_ref[step, (2 - j) * 3 * LANES : (3 - j) * 3 * LANES] = terms
            spread_ref[step, :, j * LANES : (j + 1) * LANES] = terms


def once_kernel(array_ref, *refs):
    pass


def once(array, *tokens):
    return pl.pallas_call(
        once_kernel,
        name="once",
        out_shape=jax.ShapeDtypeStruct(array.shape, array.dtype),
        in_specs=[pl.BlockSpec(memory_space=pl.ANY)] * (1 + len(tokens)),
        out_specs=pl.BlockSpec(memory_space=pl.ANY),
        input_output_aliases={0: 0},
    )(array, *tokens)


def factor_kernel(power_ref, add_ref, spread_ref, token_ref):
    token_ref[...] = jnp.zeros((8, LANES), jnp.float32)
    for step in range(LEVELS // 2):
        one, two = power_ref[2 * step], power_ref[2 * step + 1]
        for j, power in enumerate((one, two, dot(one, two))):
            terms = tall(power)
            add_ref[step, (2 - j) * 3 * LANES : (3 - j) * 3 * LANES] = terms
            spread_ref[step, :, j * LANES : (j + 1) * LANES] = terms


def joined(upper, total, beside, lead, rest):
    both = dot(jnp.where(upper, beside, total), jnp.where(upper, total, beside))
    new = dot(jnp.where(upper, beside, rest), jnp.where(upper, lead, beside))
    return both, jnp.where(upper, new, lead), jnp.where(upper, rest, new)


def pair_kernel(place_ref, total_ref, got_ref, total_out, lead_out, rest_out, lead_terms, rest_terms):
    row = lax.broadcasted_iota(jnp.int32, (LANES, LANES), 0)
    column = lax.broadcasted_iota(jnp.int32, (LANES, LANES), 1)
    identity = jnp.where(row == column, 1.0, 0.0)
    upper = place_ref[1] % 2 == 1
    total, got = total_ref[...], got_ref[...]
    lead, rest = jnp.where(upper, got, identity), jnp.where(upper, identity, got)
    total_out[...] = dot(jnp.where(upper, got, total), jnp.where(upper, total, got))
    lead_out[...], rest_out[...] = lead, rest
    lead_terms[...], rest_terms[...] = tall(lead), tall(rest)


def quad_kernel(bits_ref, total_ref, one_ref, two_ref, three_ref, lead_ref, rest_ref, total_out, lead_out, rest_out, *terms):
    odd, upper = bits_ref[0] % 2 == 1, bits_ref[0] % 4 >= 2
    two, three = two_ref[...], three_ref[...]
    total, lead, rest = joined(odd, total_ref[...], one_ref[...], lead_ref[...], rest_ref[...])
    terms[0][...], terms[1][...] = tall(lead), tall(rest)
    beside = dot(jnp.where(odd, three, two), jnp.where(odd, two, three))
    total, lead, rest = joined(upper, total, beside, lead, rest)
    terms[2][...], terms[3][...] = tall(lead), tall(rest)
    total_out[...], lead_out[...], rest_out[...] = total, lead, rest


def mask_kernel(place_ref, kept_ref, own_ref, other_ref, plane_ref, mask_ref):
    x, z, c = place_ref[0], place_ref[2], place_ref[3]
    width = NY * LANES
    kept = kept_ref[...].astype(jnp.bfloat16)
    block = lax.broadcasted_iota(jnp.int32, (LANES, width // 2), 0)
    lane = lax.broadcasted_iota(jnp.int32, (LANES, width // 2), 1) // (LANES // 2)
    source = lax.broadcasted_iota(jnp.int32, (width, width // 2), 0)
    target = lax.broadcasted_iota(jnp.int32, (width, width // 2), 1)
    picks = [
        jnp.where(source == target // 32 * 64 + target % 32 + 32 * side, 1.0, 0.0).astype(jnp.bfloat16)
        for side in range(2)
    ]
    for r in range(NX):
        lanes = slice(r * width // 2, (r + 1) * width // 2)
        own, other = own_ref[:, lanes], other_ref[:, lanes]
        whole = jnp.concatenate([jnp.where(c == 0, own, other), jnp.where(c == 0, other, own)], 1)
        for side in range(2):
            plane_ref[side * LANES : (side + 1) * LANES, lanes] = jnp.dot(
                whole, picks[side], preferred_element_type=jnp.float32
            ).astype(jnp.bfloat16)
        spread = jnp.where(block == (x ^ r) * (NZ * NY) + z * NY + lane, 1.0, 0.0).astype(jnp.bfloat16)
        mask_ref[:, lanes] = jnp.dot(kept, spread, preferred_element_type=jnp.float32)


def rows_kernel(place_ref, mask_ref, plane_ref, got_ref, out_ref, token_ref):
    x = place_ref[0]
    token_ref[...] = jnp.zeros((8, LANES), jnp.float32)
    rows = plane_ref.shape[1] // NX
    side = LANES // 2
    left = lax.broadcasted_iota(jnp.int32, (LANES, LANES), 1) < side
    for k in range(NZ):
        weights = plane_ref[...] * mask_ref[k : k + 1, :].astype(jnp.bfloat16)
        readings = jnp.concatenate([got_ref[:, x ^ r, k].reshape(rows, LANES) for r in range(NX)], 0)
        both = jnp.dot(weights, readings, preferred_element_type=jnp.float32)
        upper, lower = both[:LANES], both[LANES:]
        if k % 2 == 0:
            first = upper + pltpu.roll(lower, side, 1)
        else:
            second = lower + pltpu.roll(upper, side, 1)
            pair = jnp.where(left, first, second).T
            out_ref[k - 1], out_ref[k] = pair[:side], pair[side:]


def info_rows(place, masks, plane, received):
    return pl.pallas_call(
        rows_kernel,
        name="rows",
        out_shape=[f32(NZ, LANES // 2, LANES), f32(8, LANES)],
        in_specs=[SCALARS, WHOLE, WHOLE, WHOLE],
        out_specs=[WHOLE] * 2,
        cost_estimate=pl.CostEstimate(flops=1 << 28, bytes_accessed=3 << 20, transcendentals=0),
        compiler_params=pltpu.CompilerParams(vmem_limit_bytes=32 << 20),
    )(place, masks, plane, received)


def tail_kernel(place_ref, a_ref, b_ref, c_ref, d_ref, decay_ref, prior_ref, add_ref, spread_ref, *refs):
    rest_refs, (drive_ref, tail_ref, near_ref) = refs[:3], refs[3:]
    x = place_ref[0]
    rows = a_ref.shape[0]
    for r, ref in enumerate((a_ref, b_ref, c_ref, d_ref)):
        drive_ref[pl.ds(pl.multiple_of((x ^ r) * rows, rows), rows), :] = ref[...] * decay_ref[...]
    pushed = times(wide(prior_ref[...]), spread_ref[0, :, :LANES])
    drive_ref[:1] += jnp.where(place_ref[1] == 0, pushed, 0.0)
    tail = drive_ref[...]
    for step in reversed(range(LEVELS // 2)):
        n = 4**step
        terms = jnp.concatenate([wide(tail[j * n : (j + 1) * n]) for j in range(3)], 1)
        tail = times(terms, add_ref[step]) + tail[3 * n :]
    tail_ref[...] = jnp.broadcast_to(tail, (8, LANES))
    near_ref[...] = onward(place_ref[1], tail, jnp.broadcast_to(tail, (NK, LANES)), 1, [ref[...] for ref in rest_refs])


def onward(k, tail, sends, level, factors):
    to = lax.broadcasted_iota(jnp.int32, (NK, LANES), 0) ^ k
    terms = wide(tail)
    for step, factor in enumerate(factors):
        sends = jnp.where(to >= 2 ** (level + step), times(terms, factor), sends)
    return sends


def far_kernel(place_ref, one_ref, two_ref, three_ref, lead_ref, rest_ref, tail_ref, near_ref, four_ref, five_ref, send_ref):
    odd, upper = place_ref[2] % 2 == 1, place_ref[2] % 4 >= 2
    one, two, three = one_ref[...], two_ref[...], three_ref[...]
    lead, rest = lead_ref[...], rest_ref[...]
    beside = times(wide(jnp.where(odd, three, two)), tall(jnp.where(odd, two, three)))
    new = times(wide(jnp.where(odd, one, rest)), tall(jnp.where(odd, lead, one)))
    lead, rest = jnp.where(odd, new, lead), jnp.where(odd, rest, new)
    four_ref[...] = tall(lead)
    factors = [tall(rest)]
    new = times(wide(jnp.where(upper, beside, rest)), tall(jnp.where(upper, lead, beside)))
    five_ref[...] = tall(jnp.where(upper, new, lead))
    factors.append(tall(jnp.where(upper, rest, new)))
    send_ref[...] = onward(place_ref[1], tail_ref[:1], near_ref[...], 4, factors)


def sweep_kernel(drive_ref, spread_ref, out_ref):
    swept = drive_ref[...]
    row = lax.broadcasted_iota(jnp.int32, (STEPS, LANES), 0)
    for step in range(LEVELS // 2):
        for side in range(2):
            shift = 4**step * (1 + side)
            before = jnp.where(row >= shift, pltpu.roll(swept, shift, 0), 0.0)
            swept += times(wide(before), spread_ref[step, :, side * LANES : (side + 1) * LANES])
    out_ref[...] = swept


def step_kernel(power_ref, *refs):
    step = power_ref[...]
    for lead_ref, out_ref in zip(refs[: SCAN - 1], refs[SCAN - 1 :]):
        lead = lead_ref[:LANES].astype(jnp.float32) + lead_ref[2 * LANES :].astype(jnp.float32)
        out_ref[...] = tall(dot(lead, step))


def state_kernel(place_ref, offsets_ref, spread_ref, swept_ref, *refs):
    lead_refs, out_ref = refs[:-1], refs[-1]
    k = place_ref[1]
    index = lax.broadcasted_iota(jnp.int32, (NK, LANES), 0)
    apart = jnp.where(index < k, index ^ k, 0)
    offsets = offsets_ref[...]
    parts = []
    for level in range(SCAN):
        chosen = (apart >= 2**level) & (apart < 2 ** (level + 1))
        parts.append(jnp.sum(jnp.where(chosen, offsets, 0.0), 0, keepdims=True))
    grown = times(wide(parts[0]), spread_ref[0, :, :LANES])
    for level in range(1, SCAN):
        grown += times(wide(parts[level]), lead_refs[level - 1][...])
    for step in range(LEVELS // 2):
        more = times(wide(grown), spread_ref[step])
        grown = jnp.concatenate([grown] + [more[:, j * LANES : (j + 1) * LANES] for j in range(3)], 0)
    out_ref[...] = swept_ref[...] + grown


def on_device(observations, sensor_map, noise_precision, availability, decay_rate, prior_mean):
    modes = sensor_map.shape[1]
    rows = observations.shape[0]
    z, y, c, x = (lax.axis_index(a) for a in "zycx")
    k = (z * NY + y) * NC + c
    place = jnp.stack([x, k, z, c, y]).astype(jnp.int32)
    square = f32(modes, modes)
    packet = pack(availability, noise_precision, sensor_map)
    packets = [packet] + [xor_over_x(packet, d) for d in (1, 2, 3)]
    kept, half = gather(place, packets)
    sent = once(by_taker(observations), *packets[1:])
    received = lax.all_to_all(sent, ("y", "c", "x"), split_axis=0, concat_axis=0, tiled=True)

    for flip in (1, 2, 4):
        kept = kept + lax.ppermute(kept, "z", [(i, i ^ flip) for i in range(NZ)])
    plane, masks = local(
        mask_kernel, "masks", [place], [kept, half, lax.ppermute(half, "c", [(0, 1), (1, 0)])],
        [jax.ShapeDtypeStruct((2 * modes, NX * NY * modes // 2), jnp.bfloat16), f32(NZ, NX * NY * modes // 2)], 1 << 20,
    )

    info = weigh(availability, noise_precision, sensor_map)
    infos = [info] + [xor_over_x(info, d) for d in (1, 2, 3)]

    partial, done = info_rows(place, masks, plane, received.reshape(NY * NC, NX, NZ, rows // 2, LANES))
    partial = lax.all_to_all(partial, "z", split_axis=0, concat_axis=0, tiled=True)
    piece = jnp.sum(partial, 0)
    pieces = [piece] + [xor_over_x(piece, d) for d in (1, 2, 3)]

    retain = jnp.exp(-decay_rate)
    powers, total = local(
        power_kernel, "powers", [],
        infos + [decay_rate[None, :], jnp.broadcast_to(retain[:, None], (modes, modes))],
        [f32(LEVELS, modes, modes), square], 4 * 10**10, tokens=[done],
    )
    steps = LEVELS // 2
    adding, spreading, ready = local(
        factor_kernel, "factors", [], [powers],
        [
            jax.ShapeDtypeStruct((steps, 9 * modes, modes), jnp.bfloat16),
            jax.ShapeDtypeStruct((steps, 3 * modes, 3 * modes), jnp.bfloat16),
            f32(8, modes),
        ],
        4 * 6 * 2 * modes**3,
    )
    terms = jax.ShapeDtypeStruct((3 * modes, modes), jnp.bfloat16)
    got = lax.ppermute(total, "c", [(0, 1), (1, 0)])
    total, lead, rest, *pair_terms = local(
        pair_kernel, "pairs", [place], [total, got], [square] * 3 + [terms] * 2, 6 * 2 * modes**3
    )
    leads, rests = [pair_terms[0]], [pair_terms[1]]
    got = [lax.ppermute(total, "y", [(i, i ^ d) for i in range(NY)]) for d in (1, 2, 3)]
    total, lead, rest, *quad_terms = local(
        quad_kernel, "quads", [y.astype(jnp.int32)[None]], [total] + got + [lead, rest],
        [square] * 3 + [terms] * 4, 5 * 6 * 2 * modes**3, tokens=[ready],
    )
    leads += quad_terms[::2]
    rests += quad_terms[1::2]
    got = [lax.ppermute(total, "z", [(i, i ^ d) for i in range(NZ)]) for d in (1, 2, 3)]

    drive, tail, near = local(
        tail_kernel, "tail", [place],
        pieces + [decay_rate[None, :], prior_mean[None, :], adding, spreading] + rests,
        [f32(STEPS, modes), f32(8, modes), f32(NK, modes)], 8 * 6 * 2 * modes**3,
    )
    *far_terms, sends = local(
        far_kernel, "far", [place], got + [lead, rest, tail, near],
        [terms] * 2 + [f32(NK, modes)], 5 * 6 * 2 * modes**3,
    )
    leads += far_terms

    offsets = lax.all_to_all(sends, ("z", "y", "c"), split_axis=0, concat_axis=0, tiled=True)
    (swept,) = local(
        sweep_kernel, "sweep", [], [drive, spreading], [f32(STEPS, modes)], 8 * 12 * 2 * modes**3
    )
    leads = list(local(
        step_kernel, "steps", [], [powers[0]] + leads, [terms] * (SCAN - 1), 5 * 6 * 2 * modes**3, tokens=[swept]
    ))
    (states,) = local(
        state_kernel, "states", [place], [offsets, spreading, swept] + leads,
        [f32(STEPS, modes)], 15 * 6 * 2 * modes**3,
    )
    return states


def solution(mesh):
    fine = Mesh(mesh.devices.reshape(NZ, NY, NC, NX), ("z", "y", "c", "x"))
    return jax.shard_map(
        on_device,
        mesh=fine,
        in_specs=(
            P(("x", "z", "y", "c"), None),
            P("x", None),
            P("x", None, None),
            P(("z", "y", "c"), "x"),
            P(),
            P(),
        ),
        out_specs=P(("z", "y", "c"), None),
        check_vma=False,
    )
```
